32 devices in a mesh: groups: 2 (over x), ty: 4 (over y, core), tx: 4 (over z).
Axes of the slice: x: 2, y: 2, z: 4, core: 2. Of those that a mesh axis runs over, the one named last changes fastest.
Arguments:
- object_planes: float32 [4, 2048, 1024], P(None, ('groups', 'ty'), 'tx'), parts along dimension 1, may hold values from -5 to 5
- probe: float32 [2, 256, 256], replicated, may hold values from -5 to 5
- phase: float32 [256, 256], replicated, may hold values from -3.140625 to 3.140625
- coords: int32 [8, 4, 4, 2], P(('groups', 'ty'), 'tx'), parts along dimension 0, may hold values from 0 to 255
- live: int32 [8, 4], P(('groups', 'ty'), 'tx'), parts along dimension 0, may hold values from 0 to 4, as said below
- amplitude: float32 [8, 4, 4, 256, 256], P(('groups', 'ty'), 'tx'), parts along dimension 0, may hold values from 0 to 2
Outputs:
- updated: float32 [4, 2048, 1024], P(None, ('groups', 'ty'), 'tx'), parts along dimension 1
The draws below stay inside these ranges and needn't reach their ends.
There are 2 independent parts, one for each index of `groups`. The reference program is written for one: setup_inputs(seed, part) draws one part's arguments, and reference() takes and returns one part's arrays. A program takes and returns all parts, laid end to end along the dimension named above; an argument that names none is the same for every part. Nothing has to cross between parts.
Inputs may be any that keep to these rules, and one draw needn't show every extreme that they name: Only slots below live of their tile are used; some tile holds 4 live slots.
All inputs are finite; a program needn't handle non-finite values.
Results may differ from the reference program's by a relative error of at most 0.0003.
Values sent between devices are 32-bit elements; how exact they have to be, the bound alone decides.
No kernel may reach another device: no remote copies, remote signals or barrier semaphores. Data moves between devices by JAX's collectives and lax.ppermute only.
A program may use at most 128 MiB of HBM per device.

```python
import math
import jax
import jax.numpy as jnp
from jax import lax

W = 256
SLOTS = 4
TILES_Y = 4
TILES_X = 4
NH = 1024
NW = 1024


def draw_live(key, part):
    key_base, key_cols, key_start = jax.random.split(key, 3)
    base_load = jax.random.randint(key_base, (TILES_Y, TILES_X), 0, 3)
    dense_cols = jax.random.randint(key_cols, (2,), 0, TILES_X)
    start_row = jax.random.randint(key_start, (), 0, TILES_Y)
    row_hit = (jnp.arange(TILES_Y) - start_row) % TILES_Y < max(TILES_Y // 4, 1)
    col_hit = jnp.any(jnp.arange(TILES_X)[None, :] == dense_cols[:, None], axis=0)
    dense = row_hit[:, None] & col_hit[None, :]
    return jnp.where(dense, SLOTS, base_load).astype(jnp.int32)


def touch_ends(array, key, smallest, high):
    longest = array.shape.index(max(array.shape))
    spots = []
    for shift in (0, 1):
        where = [jax.random.randint(jax.random.fold_in(key, axis), (), 0, length) for axis, length in enumerate(array.shape)]
        where[longest] = (where[longest] + shift) % array.shape[longest]
        spots.append(tuple(where))
    return array.at[spots[0]].set(smallest).at[spots[1]].set(high)


def level_of(key, dims, shards, smallest, top_value):
    def one(axis_at, blocks):
        draws = jax.random.uniform(jax.random.fold_in(jax.random.fold_in(key, 6), axis_at), (blocks,), jnp.float32, smallest / len(shards), top_value / len(shards))
        return jnp.repeat(jnp.exp(draws), dims[axis_at] // blocks).reshape((-1,) + (1,) * (len(dims) - axis_at - 1))

    gain = one(*shards[0])
    for cut in shards[1:]:
        gain = gain * one(*cut)
    return gain


def noise(rng, shape, deviation, bound, pieces=(), kind=jnp.bfloat16):
    loudness = level_of(rng, shape, pieces, -0.22, 0.18) if pieces else 1.0
    values = jax.random.normal(rng, shape, jnp.float32) * deviation * loudness
    return jnp.minimum(jnp.maximum(values, -bound), bound).astype(kind)


def setup_inputs(seed: int = 0, part: int = 0) -> dict:
    seeds = jax.random.split(jax.random.key(seed), 7)
    part_keys = jax.random.split(jax.random.fold_in(seeds[6], part), 7)
    return {
        "object_planes": noise(part_keys[0], (4, NH, NW), 0.7, 5.0, ((1, 4), (2, 4)), jnp.float32),
        "probe": noise(seeds[1], (2, W, W), 0.7, 5.0, (), jnp.float32),
        "phase": jnp.clip(jax.random.uniform(seeds[2], (W, W), jnp.float32, -3.140625, 3.140625), -3.140625, 3.140625),
        "coords": touch_ends(jax.random.randint(part_keys[3], (TILES_Y, TILES_X, SLOTS, 2), 0, W), jax.random.fold_in(part_keys[3], 1), 0, W - 1).astype(jnp.int32),
        "live": draw_live(jax.random.fold_in(jax.random.fold_in(seeds[6], part), 71), part),
        "amplitude": jnp.clip(2.0 * jax.random.uniform(part_keys[5], (TILES_Y, TILES_X, SLOTS, W, W), jnp.float32) ** level_of(part_keys[5], (TILES_Y, TILES_X, SLOTS, W, W), ((0, 4), (1, 4)), -0.2, 0.2), 0.0, 2.0),
    }


HIGH = lax.Precision.HIGHEST

def dft_tables(probe_width):
    index_grid = jnp.arange(probe_width, dtype=jnp.int32)[:, None] * jnp.arange(probe_width, dtype=jnp.int32)[None, :] % probe_width
    angles = index_grid.astype(jnp.float32) * (2.0 * math.pi / probe_width)
    norm_scale = 1.0 / math.sqrt(probe_width)
    return (jnp.cos(angles) * norm_scale, -jnp.sin(angles) * norm_scale)

def product(left_mat, right_mat):
    return jnp.dot(left_mat, right_mat, precision=HIGH, preferred_element_type=jnp.float32)

def transform(real_part, imag_part, cos_table, sin_table):
    left_r = product(cos_table, real_part) - product(sin_table, imag_part)
    left_i = product(cos_table, imag_part) + product(sin_table, real_part)
    out_r = product(left_r, cos_table) - product(left_i, sin_table)
    out_i = product(left_r, sin_table) + product(left_i, cos_table)
    return (out_r, out_i)

def slot_terms(probe, phase_r, phase_i, cos_table, sin_table, patch, amp_plane):
    probe_r, probe_i = (probe[0], probe[1])
    first_r, first_i, second_r, second_i = (patch[0], patch[1], patch[2], patch[3])
    wave_one_r = probe_r * first_r - probe_i * first_i
    wave_one_i = probe_r * first_i + probe_i * first_r
    spec_r, spec_i = transform(wave_one_r, wave_one_i, cos_table, sin_table)
    moved_r = spec_r * phase_r - spec_i * phase_i
    moved_i = spec_r * phase_i + spec_i * phase_r
    wave_two_r, wave_two_i = transform(moved_r, moved_i, cos_table, -sin_table)
    exit_r = wave_two_r * second_r - wave_two_i * second_i
    exit_i = wave_two_r * second_i + wave_two_i * second_r
    far_r, far_i = transform(exit_r, exit_i, cos_table, sin_table)
    ratio = amp_plane / jnp.maximum(jnp.sqrt(far_r * far_r + far_i * far_i), 0.5) - 1.0
    back_r, back_i = transform(far_r * ratio, far_i * ratio, cos_table, -sin_table)
    grad_two_r = wave_two_r * back_r + wave_two_i * back_i
    grad_two_i = wave_two_r * back_i - wave_two_i * back_r
    inner_r = second_r * back_r + second_i * back_i
    inner_i = second_r * back_i - second_i * back_r
    turn_r, turn_i = transform(inner_r, inner_i, cos_table, sin_table)
    undo_r = turn_r * phase_r + turn_i * phase_i
    undo_i = turn_i * phase_r - turn_r * phase_i
    prior_r, prior_i = transform(undo_r, undo_i, cos_table, -sin_table)
    grad_one_r = probe_r * prior_r + probe_i * prior_i
    grad_one_i = probe_r * prior_i - probe_i * prior_r
    power_two = wave_two_r * wave_two_r + wave_two_i * wave_two_i
    return jnp.stack([grad_one_r, grad_one_i, grad_two_r, grad_two_i, power_two])

def reference(object_planes, probe, phase, coords, live, amplitude):
    probe_width = probe.shape[-1]
    cos_table, sin_table = dft_tables(probe_width)
    phase_r, phase_i = (jnp.cos(phase), jnp.sin(phase))
    padded = jnp.pad(object_planes, ((0, 0), (0, probe_width), (0, probe_width)))
    totals = jnp.zeros((6,) + padded.shape[1:], jnp.float32)
    probe_power = probe[0] * probe[0] + probe[1] * probe[1]
    tiles_rows, tiles_cols, slot_count = (coords.shape[0], coords.shape[1], coords.shape[2])
    flat_coords = coords.reshape(-1, 2)
    flat_amp = amplitude.reshape(-1, probe_width, probe_width)
    tile_row = jnp.repeat(jnp.arange(tiles_rows, dtype=jnp.int32), tiles_cols * slot_count)
    tile_col = jnp.tile(jnp.repeat(jnp.arange(tiles_cols, dtype=jnp.int32), slot_count), tiles_rows)
    slot_ids = jnp.tile(jnp.arange(slot_count, dtype=jnp.int32), tiles_rows * tiles_cols)
    active = slot_ids < live.reshape(-1)[tile_row * tiles_cols + tile_col]

    def accumulate(totals, slot_data):
        where_yx, amp_plane, row_tile, col_tile, is_live = slot_data
        top_row = (row_tile * probe_width + where_yx[0]).astype(jnp.int32)
        left_col = (col_tile * probe_width + where_yx[1]).astype(jnp.int32)
        zero_index = jnp.int32(0)
        patch = lax.dynamic_slice(padded, (zero_index, top_row, left_col), (4, probe_width, probe_width))

        def compute():
            gradients = slot_terms(probe, phase_r, phase_i, cos_table, sin_table, patch, amp_plane)
            return jnp.concatenate([gradients[0:2], probe_power[None], gradients[2:5]])

        def skip():
            return jnp.zeros((6, probe_width, probe_width), jnp.float32)
        contrib = lax.cond(is_live, compute, skip)
        current = lax.dynamic_slice(totals, (zero_index, top_row, left_col), (6, probe_width, probe_width))
        return (lax.dynamic_update_slice(totals, current + contrib, (zero_index, top_row, left_col)), None)
    totals, _ = lax.scan(accumulate, totals, (flat_coords, flat_amp, tile_row, tile_col, active))
    totals = totals[:, :object_planes.shape[1], :object_planes.shape[2]]
    first = object_planes[0:2] + totals[0:2] / (totals[2:3] + 1.0)
    second = object_planes[2:4] + totals[3:5] / (totals[5:6] + 1.0)
    return jnp.concatenate([first, second])
```

```python
import functools
import math

import jax
import jax.numpy as jnp
import ml_dtypes
import numpy as np
from jax import lax
from jax.experimental import pallas as pl
from jax.experimental.pallas import tpu as pltpu
from jax.sharding import PartitionSpec as P

F32 = jnp.float32
BF16 = jnp.bfloat16
VMEM = pl.BlockSpec(memory_space=pltpu.VMEM)
SMEM = pl.BlockSpec(memory_space=pltpu.SMEM)


def from_behind(block, axis, distance):
    devices = range(lax.axis_size(axis))
    route = [(i - distance, i) for i in devices if i - distance in devices]
    return lax.ppermute(block, axis, route)


def from_diagonal(block, distance):
    rows, cols = lax.axis_size("ty"), lax.axis_size("tx")
    route = [
        ((i - distance) * cols + j - distance, i * cols + j)
        for i in range(rows)
        for j in range(cols)
        if 0 <= i - distance < rows and 0 <= j - distance < cols
    ]
    return lax.ppermute(block, ("ty", "tx"), route)


def transform_tables(width):
    half = width // 2
    n = np.arange(half)[:, None]
    k = np.arange(half)[None, :]
    out = []
    for odd in (0, 1):
        angle = -2.0 * math.pi * ((n * (2 * k + odd)) % width) / width
        wr, wi = np.cos(angle) / math.sqrt(width), np.sin(angle) / math.sqrt(width)
        real = np.block([[wr, wi], [-wi, wr]])
        head = real.astype(ml_dtypes.bfloat16)
        tail = (real - head.astype(np.float64)).astype(ml_dtypes.bfloat16)
        out += [head, tail]
    out += [np.ascontiguousarray(m.T) for m in out]
    return np.stack(out)


def order_table(width):
    half = width // 2
    table = np.zeros((2, width, width), np.float32)
    source = np.concatenate([np.arange(0, width, 2), np.arange(1, width, 2)])
    table[0, np.arange(width), source] = 1.0
    table[1] = table[0].T
    return table


def split(x):
    head = x.astype(BF16)
    return head, (x - head.astype(F32)).astype(BF16)


def mm(a, b):
    return jnp.dot(a, b, preferred_element_type=F32)


def right_mul(x, table, at):
    head, tail = split(x)
    return mm(head, table[at]) + mm(tail, table[at]) + mm(head, table[at + 1])


def left_mul(x, table, at):
    head, tail = split(x)
    return mm(table[at], head) + mm(table[at], tail) + mm(table[at + 1], head)


def forward(xr, xi, table):
    half = xr.shape[0] // 2
    sr = jnp.concatenate([xr[:half] + xr[half:], xi[:half] + xi[half:]])
    dr = jnp.concatenate([xr[:half] - xr[half:], xi[:half] - xi[half:]])
    even = left_mul(sr, table, 4)
    odd = left_mul(dr, table, 6)
    yr = jnp.concatenate([even[:half], odd[:half]])
    yi = jnp.concatenate([even[half:], odd[half:]])
    sr = jnp.concatenate([yr[:, :half] + yr[:, half:], yi[:, :half] + yi[:, half:]], axis=1)
    dr = jnp.concatenate([yr[:, :half] - yr[:, half:], yi[:, :half] - yi[:, half:]], axis=1)
    even = right_mul(sr, table, 0)
    odd = right_mul(dr, table, 2)
    return (
        jnp.concatenate([even[:, :half], odd[:, :half]], axis=1),
        jnp.concatenate([even[:, half:], odd[:, half:]], axis=1),
    )


def backward(xr, xi, table):
    half = xr.shape[0] // 2
    even = left_mul(jnp.concatenate([xr[:half], xi[:half]]), table, 0)
    odd = left_mul(jnp.concatenate([xr[half:], xi[half:]]), table, 2)
    yr = jnp.concatenate([even[:half] + odd[:half], even[:half] - odd[:half]])
    yi = jnp.concatenate([even[half:] + odd[half:], even[half:] - odd[half:]])
    even = right_mul(jnp.concatenate([yr[:, :half], yi[:, :half]], axis=1), table, 4)
    odd = right_mul(jnp.concatenate([yr[:, half:], yi[:, half:]], axis=1), table, 6)
    return (
        jnp.concatenate([even[:, :half] + odd[:, :half], even[:, :half] - odd[:, :half]], axis=1),
        jnp.concatenate([even[:, half:] + odd[:, half:], even[:, half:] - odd[:, half:]], axis=1),
    )


def wraps(shape, top, left):
    rows = lax.broadcasted_iota(jnp.int32, shape, 0)
    cols = lax.broadcasted_iota(jnp.int32, shape, 1)
    return rows < top, cols < left


def pick(quads, plane, low, right):
    own, east, south, corner = (q[plane] for q in quads)
    return jnp.where(low, jnp.where(right, corner, south), jnp.where(right, east, own))


def deposit(quads, plane, value, low, right):
    own, east, south, corner = quads
    zero = jnp.zeros_like(value)
    upper = jnp.where(low, zero, value)
    lower = jnp.where(low, value, zero)
    own[plane] += jnp.where(right, zero, upper)
    east[plane] += jnp.where(right, upper, zero)
    south[plane] += jnp.where(right, zero, lower)
    corner[plane] += jnp.where(right, lower, zero)


def clear(refs):
    for ref in refs:
        ref[...] = jnp.zeros_like(ref)


def prep_kernel(info, probe, amp, phasor, order, shifted, amp_out, phasor_out):
    slots = amp.shape[0]

    def reorder(x):
        once = jnp.dot(x, order[1], precision=lax.Precision.HIGHEST, preferred_element_type=F32)
        return jnp.dot(order[0], once, precision=lax.Precision.HIGHEST, preferred_element_type=F32)

    for part in range(2):
        phasor_out[part] = reorder(phasor[part])

    def body(s, carry):
        top, left = info[0, 2 * s], info[0, 2 * s + 1]
        for part in range(2):
            shifted[s, part] = pltpu.roll(pltpu.roll(probe[part], top, 0), left, 1)
        amp_out[s] = reorder(amp[s])
        return carry

    lax.fori_loop(0, info[0, 2 * slots], body, 0)


def cover_kernel(info, probe, cover):
    slots = (info.shape[1] - 1) // 2
    cover[...] = jnp.zeros_like(cover)
    for tile in range(4):

        def body(s, carry, tile=tile):
            top, left = info[tile, 2 * s], info[tile, 2 * s + 1]
            power = probe[0] * probe[0] + probe[1] * probe[1]
            moved = pltpu.roll(pltpu.roll(power, top, 0), left, 1)
            low, right = wraps(power.shape, top, left)
            keep = (low if tile >= 2 else ~low) & (right if tile % 2 else ~right)
            cover[...] += jnp.where(keep, moved, 0.0)
            return carry

        lax.fori_loop(0, info[tile, 2 * slots], body, 0)


def first_kernel(info, own, east, south, corner, shifted, phasor, table, wave, p_own, p_east, p_south, p_corner):
    slots = shifted.shape[0]
    quads_in = (own, east, south, corner)
    quads = (p_own, p_east, p_south, p_corner)
    clear(quads)

    def body(s, carry):
        low, right = wraps(own.shape[1:], info[0, 2 * s], info[0, 2 * s + 1])
        fr, fi = pick(quads_in, 0, low, right), pick(quads_in, 1, low, right)
        pr, pi = shifted[s, 0], shifted[s, 1]
        ur, ui = forward(pr * fr - pi * fi, pr * fi + pi * fr, table)
        hr, hi = phasor[0], phasor[1]
        wr, wi = backward(ur * hr - ui * hi, ur * hi + ui * hr, table)
        wave[s, 0] = wr
        wave[s, 1] = wi
        deposit(quads, 0, wr * wr + wi * wi, low, right)
        return carry

    lax.fori_loop(0, info[0, 2 * slots], body, 0)


def second_kernel(info, own, east, south, corner, wave, amp, table, inner, g_own, g_east, g_south, g_corner):
    slots = wave.shape[0]
    quads_in = (own, east, south, corner)
    quads = (g_own, g_east, g_south, g_corner)
    clear(quads)

    def body(s, carry):
        low, right = wraps(own.shape[1:], info[0, 2 * s], info[0, 2 * s + 1])
        sr, si = pick(quads_in, 0, low, right), pick(quads_in, 1, low, right)
        wr, wi = wave[s, 0], wave[s, 1]
        fr, fi = forward(wr * sr - wi * si, wr * si + wi * sr, table)
        ratio = amp[s] * lax.rsqrt(jnp.maximum(fr * fr + fi * fi, 0.25)) - 1.0
        br, bi = backward(fr * ratio, fi * ratio, table)
        inner[s, 0] = sr * br + si * bi
        inner[s, 1] = sr * bi - si * br
        deposit(quads, 0, wr * br + wi * bi, low, right)
        deposit(quads, 1, wr * bi - wi * br, low, right)
        return carry

    lax.fori_loop(0, info[0, 2 * slots], body, 0)


def third_kernel(info, inner, shifted, phasor, table, g_own, g_east, g_south, g_corner):
    slots = inner.shape[0]
    quads = (g_own, g_east, g_south, g_corner)
    clear(quads)

    def body(s, carry):
        low, right = wraps(g_own.shape[1:], info[0, 2 * s], info[0, 2 * s + 1])
        tr, ti = forward(inner[s, 0], inner[s, 1], table)
        hr, hi = phasor[0], phasor[1]
        qr, qi = backward(tr * hr + ti * hi, ti * hr - tr * hi, table)
        pr, pi = shifted[s, 0], shifted[s, 1]
        deposit(quads, 0, pr * qr + pi * qi, low, right)
        deposit(quads, 1, pr * qi - pi * qr, low, right)
        return carry

    lax.fori_loop(0, info[0, 2 * slots], body, 0)


def call(kernel, shapes, *operands, microseconds=4):
    return pl.pallas_call(
        kernel,
        out_shape=[jax.ShapeDtypeStruct(s, F32) for s in shapes],
        in_specs=[SMEM] + [VMEM] * (len(operands) - 1),
        out_specs=[VMEM] * len(shapes),
        compiler_params=pltpu.CompilerParams(vmem_limit_bytes=32 << 20),
        cost_estimate=pl.CostEstimate(
            flops=microseconds * 10**9, bytes_accessed=microseconds * 10**6, transcendentals=0
        ),
    )(*operands)


def on_device(object_planes, probe, phase, coords, live, amplitude):
    width = probe.shape[-1]
    slots = coords.shape[2]
    tile = (width, width)
    pair = (2,) + tile
    table = jnp.asarray(transform_tables(width))
    order = jnp.asarray(order_table(width))

    own_info = jnp.concatenate([coords.reshape(1, 2 * slots), live.reshape(1, 1)], axis=1)
    first, second = object_planes[0:2], object_planes[2:4]
    east1 = from_behind(first, "tx", -1)
    south1 = from_behind(first, "ty", -1)
    east2 = from_behind(second, "tx", -1)
    south2 = from_behind(second, "ty", -1)
    corner1 = from_behind(east1, "ty", -1)
    corner2 = from_behind(east2, "ty", -1)
    info = jnp.concatenate(
        [own_info, from_behind(own_info, "tx", 1), from_behind(own_info, "ty", 1), from_diagonal(own_info, 1)]
    )

    phasor = jnp.stack([jnp.cos(phase), jnp.sin(phase)])
    shifted, amp, phasor = call(
        prep_kernel, [(slots,) + pair, (slots,) + tile, pair], own_info, probe, amplitude[0, 0], phasor, order
    )
    cover = call(cover_kernel, [tile], info, probe)[0]
    wave, *power = call(
        first_kernel,
        [(slots,) + pair] + [(1,) + tile] * 4,
        own_info, first, east1, south1, corner1, shifted, phasor, table,
    )
    inner, *grad2 = call(
        second_kernel,
        [(slots,) + pair] + [pair] * 4,
        own_info, second, east2, south2, corner2, wave, amp, table,
    )
    grad1 = call(third_kernel, [pair] * 4, own_info, inner, shifted, phasor, table)

    def gather_sums(own, east, south, corner):
        moved = from_behind(corner, "ty", 1)
        return own + from_behind(south, "ty", 1) + from_behind(east + moved, "tx", 1)

    sum_power = gather_sums(*power)
    sum2 = gather_sums(*grad2)
    sum1 = gather_sums(*grad1)
    return jnp.concatenate([first + sum1 / (cover + 1.0)[None], second + sum2 / (sum_power + 1.0)])


def solution(mesh):
    return jax.shard_map(
        on_device,
        mesh=mesh,
        in_specs=(
            P(None, ("groups", "ty"), "tx"),
            P(),
            P(),
            P(("groups", "ty"), "tx", None, None),
            P(("groups", "ty"), "tx"),
            P(("groups", "ty"), "tx", None, None, None),
        ),
        out_specs=P(None, ("groups", "ty"), "tx"),
        check_vma=False,
    )
```

```python
import math

import jax
import jax.numpy as jnp
import ml_dtypes
import numpy as np
from jax import lax
from jax.experimental import pallas as pl
from jax.experimental.pallas import tpu as pltpu
from jax.sharding import PartitionSpec as P

F32 = jnp.float32
BF16 = jnp.bfloat16
VMEM = pl.BlockSpec(memory_space=pltpu.VMEM)
SMEM = pl.BlockSpec(memory_space=pltpu.SMEM)


def from_behind(block, axis, distance):
    devices = range(lax.axis_size(axis))
    route = [(i - distance, i) for i in devices if i - distance in devices]
    return lax.ppermute(block, axis, route)


def transform_tables(width):
    half = width // 2
    n = np.arange(half)[:, None]
    k = np.arange(half)[None, :]
    out = []
    for odd in (0, 1):
        angle = -2.0 * math.pi * ((n * (2 * k + odd)) % width) / width
        wr, wi = np.cos(angle) / math.sqrt(width), np.sin(angle) / math.sqrt(width)
        real = np.block([[wr, wi], [-wi, wr]])
        head = real.astype(ml_dtypes.bfloat16)
        tail = (real - head.astype(np.float64)).astype(ml_dtypes.bfloat16)
        out += [head, tail]
    out += [np.ascontiguousarray(m.T) for m in out]
    return np.stack(out)


def order_table(width):
    half = width // 2
    table = np.zeros((2, width, width), ml_dtypes.bfloat16)
    source = np.concatenate([np.arange(0, width, 2), np.arange(1, width, 2)])
    table[0, np.arange(width), source] = 1.0
    table[1] = table[0].T
    return table


def split(x):
    head = x.astype(BF16)
    return head, (x - head.astype(F32)).astype(BF16)


def mm(a, b):
    return jnp.dot(a, b, preferred_element_type=F32)


def right_mul(x, table, at):
    head, tail = split(x)
    return mm(head, table[at]) + mm(tail, table[at]) + mm(head, table[at + 1])


def left_mul(x, table, at):
    head, tail = split(x)
    return mm(table[at], head) + mm(table[at], tail) + mm(table[at + 1], head)


def stack_rows(blocks):
    return jnp.concatenate(blocks, axis=0)


def stack_cols(blocks):
    return jnp.concatenate(blocks, axis=1)


def forward(waves, table):
    half = waves[0][0].shape[0] // 2
    steps = []
    for xr, xi in waves:
        sums = stack_rows([xr[:half] + xr[half:], xi[:half] + xi[half:]])
        diffs = stack_rows([xr[:half] - xr[half:], xi[:half] - xi[half:]])
        steps.append((left_mul(sums, table, 4), left_mul(diffs, table, 6)))
    out = []
    for even, odd in steps:
        yr = stack_rows([even[:half], odd[:half]])
        yi = stack_rows([even[half:], odd[half:]])
        sums = stack_cols([yr[:, :half] + yr[:, half:], yi[:, :half] + yi[:, half:]])
        diffs = stack_cols([yr[:, :half] - yr[:, half:], yi[:, :half] - yi[:, half:]])
        out.append((right_mul(sums, table, 0), right_mul(diffs, table, 2)))
    return [
        (stack_cols([even[:, :half], odd[:, :half]]), stack_cols([even[:, half:], odd[:, half:]]))
        for even, odd in out
    ]


def backward(waves, table):
    half = waves[0][0].shape[0] // 2
    steps = []
    for xr, xi in waves:
        even = left_mul(stack_rows([xr[:half], xi[:half]]), table, 0)
        odd = left_mul(stack_rows([xr[half:], xi[half:]]), table, 2)
        steps.append((even, odd))
    out = []
    for even, odd in steps:
        yr = stack_rows([even[:half] + odd[:half], even[:half] - odd[:half]])
        yi = stack_rows([even[half:] + odd[half:], even[half:] - odd[half:]])
        even = right_mul(stack_cols([yr[:, :half], yi[:, :half]]), table, 4)
        odd = right_mul(stack_cols([yr[:, half:], yi[:, half:]]), table, 6)
        out.append((even, odd))
    return [
        tuple(
            stack_cols([even[:, part] + odd[:, part], even[:, part] - odd[:, part]])
            for part in (slice(0, half), slice(half, None))
        )
        for even, odd in out
    ]


class Window:
    def __init__(self, info, tile, slot, shape):
        slots = (info.shape[1] - 1) // 2
        rows = lax.broadcasted_iota(jnp.int32, shape, 0)
        cols = lax.broadcasted_iota(jnp.int32, shape, 1)
        self.low = rows < info[tile, 2 * slot]
        self.right = cols < info[tile, 2 * slot + 1]
        mine = self.right if tile else ~self.right
        mine = mine & (slot < info[tile, 2 * slots])
        self.keep_up = mine & ~self.low
        self.keep_low = mine & self.low

    def pick(self, quads, plane):
        own, east, south, corner = (q[plane] for q in quads)
        return jnp.where(self.low, jnp.where(self.right, corner, south), jnp.where(self.right, east, own))

    def deposit(self, up, low, plane, value):
        up[plane] += jnp.where(self.keep_up, value, 0.0)
        low[plane] += jnp.where(self.keep_low, value, 0.0)


def each_group(info, tile, body):
    slots = (info.shape[1] - 1) // 2
    group = 2 if slots % 2 == 0 else 1

    def step(g, carry):
        body([g * group + j for j in range(group)])
        return carry

    lax.fori_loop(0, (info[tile, 2 * slots] + group - 1) // group, step, 0)


def clear(*refs):
    for ref in refs:
        ref[...] = jnp.zeros_like(ref)


def prep_kernel(info, amp, phasor, order, amp_out, phasor_out):
    slots = amp.shape[0]

    def reorder(x):
        head, tail = split(x)
        once = mm(head, order[1]) + mm(tail, order[1])
        head, tail = split(once)
        return mm(order[0], head) + mm(order[0], tail)

    for part in range(2):
        phasor_out[part] = reorder(phasor[part])

    def reorder_amp(s, carry):
        amp_out[s] = reorder(amp[s])
        return carry

    lax.fori_loop(0, info[0, 2 * slots], reorder_amp, 0)


def shift_kernel(info, probe, shifted):
    slots = shifted.shape[1]
    for tile in range(2):

        def body(s, carry, tile=tile):
            top, left = info[tile, 2 * s], info[tile, 2 * s + 1]
            for part in range(2):
                shifted[tile, s, part] = pltpu.roll(pltpu.roll(probe[part], top, 0), left, 1)
            return carry

        lax.fori_loop(0, info[tile, 2 * slots], body, 0)


def first_kernel(
    info, own, east, south, corner, west, west_south, shifted, phasor, table, wave, up, low
):
    clear(up, low)
    shape = own.shape[1:]
    for tile, quads in ((0, (own, east, south, corner)), (1, (west, own, west_south, south))):

        def body(slots, tile=tile, quads=quads):
            windows = [Window(info, tile, s, shape) for s in slots]
            waves = []
            for s, w in zip(slots, windows):
                fr, fi = w.pick(quads, 0), w.pick(quads, 1)
                pr, pi = shifted[tile, s, 0], shifted[tile, s, 1]
                w.deposit(up, low, 1, pr * pr + pi * pi)
                waves.append((pr * fr - pi * fi, pr * fi + pi * fr))
            waves = forward(waves, table)
            hr, hi = phasor[0], phasor[1]
            waves = backward([(ur * hr - ui * hi, ur * hi + ui * hr) for ur, ui in waves], table)
            for s, w, (wr, wi) in zip(slots, windows, waves):
                wave[tile, s, 0] = wr
                wave[tile, s, 1] = wi
                w.deposit(up, low, 0, wr * wr + wi * wi)

        each_group(info, tile, body)


def second_step(info, tile, slots, quads, wave, amp, table, inner, up, low):
    shape = quads[0].shape[1:]
    windows = [Window(info, tile, s, shape) for s in slots]
    waves = []
    for s, w in zip(slots, windows):
        sr, si = w.pick(quads, 0), w.pick(quads, 1)
        wr, wi = wave[tile, s, 0], wave[tile, s, 1]
        waves.append((wr * sr - wi * si, wr * si + wi * sr))
    scaled = []
    for s, (fr, fi) in zip(slots, forward(waves, table)):
        ratio = amp[s] * lax.rsqrt(jnp.maximum(fr * fr + fi * fi, 0.25)) - 1.0
        scaled.append((fr * ratio, fi * ratio))
    for s, w, (br, bi) in zip(slots, windows, backward(scaled, table)):
        sr, si = w.pick(quads, 0), w.pick(quads, 1)
        wr, wi = wave[tile, s, 0], wave[tile, s, 1]
        inner[s, 0] = sr * br + si * bi
        inner[s, 1] = sr * bi - si * br
        w.deposit(up, low, 0, wr * br + wi * bi)
        w.deposit(up, low, 1, wr * bi - wi * br)


def third_step(info, tile, slots, inner, shifted, phasor, table, up, low):
    shape = up.shape[1:]
    waves = forward([(inner[s, 0], inner[s, 1]) for s in slots], table)
    hr, hi = phasor[0], phasor[1]
    waves = backward([(tr * hr + ti * hi, ti * hr - tr * hi) for tr, ti in waves], table)
    for s, (qr, qi) in zip(slots, waves):
        w = Window(info, tile, s, shape)
        pr, pi = shifted[tile, s, 0], shifted[tile, s, 1]
        w.deposit(up, low, 0, pr * qr + pi * qi)
        w.deposit(up, low, 1, pr * qi - pi * qr)


def own_kernel(
    info, own, east, south, corner, wave, amp, shifted, phasor, table, up2, low2, up1, low1, inner
):
    clear(up2, low2, up1, low1)
    quads = (own, east, south, corner)

    def body(slots):
        second_step(info, 0, slots, quads, wave, amp, table, inner, up2, low2)
        third_step(info, 0, slots, inner, shifted, phasor, table, up1, low1)

    each_group(info, 0, body)


def west_second_kernel(
    info, own, south, west, west_south, wave, amp, table, up_in, low_in, inner, up, low
):
    up[...] = up_in[...]
    low[...] = low_in[...]
    quads = (west, own, west_south, south)
    each_group(
        info, 1, lambda slots: second_step(info, 1, slots, quads, wave, amp, table, inner, up, low)
    )


def west_third_kernel(info, inner, shifted, phasor, table, up_in, low_in, up, low):
    up[...] = up_in[...]
    low[...] = low_in[...]
    each_group(
        info, 1, lambda slots: third_step(info, 1, slots, inner, shifted, phasor, table, up, low)
    )


def call(kernel, shapes, *operands, scratch=(), microseconds=4):
    return pl.pallas_call(
        kernel,
        out_shape=[pltpu.VMEM(s, F32) for s in shapes],
        in_specs=[SMEM] + [VMEM] * (len(operands) - 1),
        out_specs=[VMEM] * len(shapes),
        scratch_shapes=[pltpu.VMEM(s, F32) for s in scratch],
        compiler_params=pltpu.CompilerParams(vmem_limit_bytes=20 << 20),
        cost_estimate=pl.CostEstimate(
            flops=microseconds * 10**9, bytes_accessed=microseconds * 10**6, transcendentals=0
        ),
    )(*operands)


def on_device(object_planes, probe, phase, coords, live, amplitude):
    width = probe.shape[-1]
    slots = coords.shape[2]
    tile = (width, width)
    pair = (2,) + tile
    table = jnp.asarray(transform_tables(width))
    order = jnp.asarray(order_table(width))

    own_info = jnp.concatenate([coords.reshape(1, 2 * slots), live.reshape(1, 1)], axis=1)
    first, second = object_planes[0:2], object_planes[2:4]
    info = jnp.concatenate([own_info, from_behind(own_info, "tx", 1)])
    east1 = from_behind(first, "tx", -1)
    west1 = from_behind(first, "tx", 1)
    south1 = from_behind(first, "ty", -1)
    east2 = from_behind(second, "tx", -1)
    west2 = from_behind(second, "tx", 1)
    south2 = from_behind(second, "ty", -1)
    phasor = jnp.stack([jnp.cos(phase), jnp.sin(phase)])
    amp, phasor = call(prep_kernel, [(slots,) + tile, pair], own_info, amplitude[0, 0], phasor, order)
    amp_west = from_behind(amp, "tx", 1)
    shifted = call(shift_kernel, [(2, slots) + pair], info, probe)[0]

    corner1 = from_behind(east1, "ty", -1)
    west_south1 = from_behind(west1, "ty", -1)
    corner2 = from_behind(east2, "ty", -1)
    west_south2 = from_behind(west2, "ty", -1)

    wave, power_up, power_low = call(
        first_kernel,
        [(2, slots) + pair, pair, pair],
        info, first, east1, south1, corner1, west1, west_south1, shifted, phasor, table,
        microseconds=10,
    )
    power_moved = from_behind(power_low, "ty", 1)
    up2, low2, up1, low1 = call(
        own_kernel,
        [pair] * 4,
        info, second, east2, south2, corner2, wave, amp, shifted, phasor, table,
        scratch=[(slots,) + pair], microseconds=10,
    )
    inner, up2, low2 = call(
        west_second_kernel,
        [(slots,) + pair, pair, pair],
        info, second, south2, west2, west_south2, wave, amp_west, table, up2, low2,
    )
    moved2 = from_behind(low2, "ty", 1)
    up1, low1 = call(
        west_third_kernel, [pair, pair], info, inner, shifted, phasor, table, up1, low1
    )
    moved1 = from_behind(low1, "ty", 1)
    power = power_up + power_moved
    return jnp.concatenate(
        [
            first + (up1 + moved1) / (power[1:2] + 1.0),
            second + (up2 + moved2) / (power[0:1] + 1.0),
        ]
    )


def solution(mesh):
    return jax.shard_map(
        on_device,
        mesh=mesh,
        in_specs=(
            P(None, ("groups", "ty"), "tx"),
            P(),
            P(),
            P(("groups", "ty"), "tx", None, None),
            P(("groups", "ty"), "tx"),
            P(("groups", "ty"), "tx", None, None, None),
        ),
        out_specs=P(None, ("groups", "ty"), "tx"),
        check_vma=False,
    )
```

```python
import math

import jax
import jax.numpy as jnp
import ml_dtypes
import numpy as np
from jax import lax
from jax.experimental import pallas as pl
from jax.experimental.pallas import tpu as pltpu
from jax.sharding import PartitionSpec as P

F32 = jnp.float32
BF16 = jnp.bfloat16
VMEM = pl.BlockSpec(memory_space=pltpu.VMEM)
COST = 0.001
COST_BIG = 0.001
SMEM = pl.BlockSpec(memory_space=pltpu.SMEM)


def from_behind(block, axis, distance):
    devices = range(lax.axis_size(axis))
    route = [(i - distance, i) for i in devices if i - distance in devices]
    return lax.ppermute(block, axis, route)


def transform_tables(width):
    half = width // 2
    n = np.arange(half)[:, None]
    k = np.arange(half)[None, :]
    out = []
    for odd in (0, 1):
        angle = -2.0 * math.pi * ((n * (2 * k + odd)) % width) / width
        wr, wi = np.cos(angle) / math.sqrt(width), np.sin(angle) / math.sqrt(width)
        real = np.block([[wr, wi], [-wi, wr]])
        head = real.astype(ml_dtypes.bfloat16)
        tail = (real - head.astype(np.float64)).astype(ml_dtypes.bfloat16)
        out += [head, tail]
    out += [np.ascontiguousarray(m.T) for m in out]
    return np.stack(out)


def order_table(width):
    half = width // 2
    table = np.zeros((2, width, width), ml_dtypes.bfloat16)
    source = np.concatenate([np.arange(0, width, 2), np.arange(1, width, 2)])
    table[0, np.arange(width), source] = 1.0
    table[1] = table[0].T
    return table


def split(x):
    head = x.astype(BF16)
    return head, (x - head.astype(F32)).astype(BF16)


def mm(a, b):
    return jnp.dot(a, b, preferred_element_type=F32)


def right_mul(x, table, at):
    head, tail = split(x)
    return mm(head, table[at]) + mm(tail, table[at]) + mm(head, table[at + 1])


def left_mul(x, table, at):
    head, tail = split(x)
    return mm(table[at], head) + mm(table[at], tail) + mm(table[at + 1], head)


def stack_rows(blocks):
    return jnp.concatenate(blocks, axis=0)


def stack_cols(blocks):
    return jnp.concatenate(blocks, axis=1)


def forward(waves, table):
    half = waves[0][0].shape[0] // 2
    steps = []
    for xr, xi in waves:
        sums = stack_rows([xr[:half] + xr[half:], xi[:half] + xi[half:]])
        diffs = stack_rows([xr[:half] - xr[half:], xi[:half] - xi[half:]])
        steps.append((left_mul(sums, table, 4), left_mul(diffs, table, 6)))
    out = []
    for even, odd in steps:
        yr = stack_rows([even[:half], odd[:half]])
        yi = stack_rows([even[half:], odd[half:]])
        sums = stack_cols([yr[:, :half] + yr[:, half:], yi[:, :half] + yi[:, half:]])
        diffs = stack_cols([yr[:, :half] - yr[:, half:], yi[:, :half] - yi[:, half:]])
        out.append((right_mul(sums, table, 0), right_mul(diffs, table, 2)))
    return [
        (stack_cols([even[:, :half], odd[:, :half]]), stack_cols([even[:, half:], odd[:, half:]]))
        for even, odd in out
    ]


def backward(waves, table):
    half = waves[0][0].shape[0] // 2
    steps = []
    for xr, xi in waves:
        even = left_mul(stack_rows([xr[:half], xi[:half]]), table, 0)
        odd = left_mul(stack_rows([xr[half:], xi[half:]]), table, 2)
        steps.append((even, odd))
    out = []
    for even, odd in steps:
        yr = stack_rows([even[:half] + odd[:half], even[:half] - odd[:half]])
        yi = stack_rows([even[half:] + odd[half:], even[half:] - odd[half:]])
        even = right_mul(stack_cols([yr[:, :half], yi[:, :half]]), table, 4)
        odd = right_mul(stack_cols([yr[:, half:], yi[:, half:]]), table, 6)
        out.append((even, odd))
    return [
        tuple(
            stack_cols([even[:, part] + odd[:, part], even[:, part] - odd[:, part]])
            for part in (slice(0, half), slice(half, None))
        )
        for even, odd in out
    ]


class Window:
    def __init__(self, info, tile, slot, shape):
        slots = (info.shape[1] - 1) // 2
        rows = lax.broadcasted_iota(jnp.int32, shape, 0)
        cols = lax.broadcasted_iota(jnp.int32, shape, 1)
        self.low = rows < info[tile, 2 * slot]
        self.right = cols < info[tile, 2 * slot + 1]
        mine = self.right if tile else ~self.right
        mine = mine & (slot < info[tile, 2 * slots])
        self.keep_up = mine & ~self.low
        self.keep_low = mine & self.low

    def pick(self, quads, plane):
        own, east, south, corner = (q[plane] for q in quads)
        return jnp.where(self.low, jnp.where(self.right, corner, south), jnp.where(self.right, east, own))

    def deposit(self, up, low, plane, value):
        up[plane] += jnp.where(self.keep_up, value, 0.0)
        low[plane] += jnp.where(self.keep_low, value, 0.0)


def each_group(info, tile, body):
    slots = (info.shape[1] - 1) // 2
    group = 2 if slots % 2 == 0 else 1

    def step(g, carry):
        body([g * group + j for j in range(group)])
        return carry

    lax.fori_loop(0, (info[tile, 2 * slots] + group - 1) // group, step, 0)


def clear(*refs):
    for ref in refs:
        ref[...] = jnp.zeros_like(ref)


def prep_kernel(info, amp, phasor, order, amp_out, phasor_out):
    slots = amp.shape[0]

    def reorder(x):
        head, tail = split(x)
        once = mm(head, order[1]) + mm(tail, order[1])
        head, tail = split(once)
        return mm(order[0], head) + mm(order[0], tail)

    for part in range(2):
        phasor_out[part] = reorder(phasor[part])

    def reorder_amp(s, carry):
        amp_out[s] = reorder(amp[s])
        return carry

    lax.fori_loop(0, info[0, 2 * slots], reorder_amp, 0)


def shift_kernel(info, probe, shifted):
    slots = shifted.shape[1]
    for tile in range(2):

        def body(s, carry, tile=tile):
            top, left = info[tile, 2 * s], info[tile, 2 * s + 1]
            for part in range(2):
                shifted[tile, s, part] = pltpu.roll(pltpu.roll(probe[part], top, 0), left, 1)
            return carry

        lax.fori_loop(0, info[tile, 2 * slots], body, 0)


def first_kernel(
    info, own, east, south, corner, west, west_south, shifted, phasor, table, wave, up, low
):
    clear(up, low)
    shape = own.shape[1:]
    south = south.at[0:2]
    for tile, quads in ((0, (own, east, south, corner)), (1, (west, own, west_south, south))):

        def body(slots, tile=tile, quads=quads):
            windows = [Window(info, tile, s, shape) for s in slots]
            waves = []
            for s, w in zip(slots, windows):
                fr, fi = w.pick(quads, 0), w.pick(quads, 1)
                pr, pi = shifted[tile, s, 0], shifted[tile, s, 1]
                w.deposit(up, low, 1, pr * pr + pi * pi)
                waves.append((pr * fr - pi * fi, pr * fi + pi * fr))
            waves = forward(waves, table)
            hr, hi = phasor[0], phasor[1]
            waves = backward([(ur * hr - ui * hi, ur * hi + ui * hr) for ur, ui in waves], table)
            for s, w, (wr, wi) in zip(slots, windows, waves):
                wave[tile, s, 0] = wr
                wave[tile, s, 1] = wi
                w.deposit(up, low, 0, wr * wr + wi * wi)

        each_group(info, tile, body)


def second_step(info, tile, slots, quads, wave, amp, table, inner, up, low):
    shape = quads[0].shape[1:]
    windows = [Window(info, tile, s, shape) for s in slots]
    waves = []
    for s, w in zip(slots, windows):
        sr, si = w.pick(quads, 0), w.pick(quads, 1)
        wr, wi = wave[tile, s, 0], wave[tile, s, 1]
        waves.append((wr * sr - wi * si, wr * si + wi * sr))
    scaled = []
    for s, (fr, fi) in zip(slots, forward(waves, table)):
        ratio = amp[s] * lax.rsqrt(jnp.maximum(fr * fr + fi * fi, 0.25)) - 1.0
        scaled.append((fr * ratio, fi * ratio))
    for s, w, (br, bi) in zip(slots, windows, backward(scaled, table)):
        sr, si = w.pick(quads, 0), w.pick(quads, 1)
        wr, wi = wave[tile, s, 0], wave[tile, s, 1]
        inner[s, 0] = sr * br + si * bi
        inner[s, 1] = sr * bi - si * br
        w.deposit(up, low, 0, wr * br + wi * bi)
        w.deposit(up, low, 1, wr * bi - wi * br)


def third_step(info, tile, slots, inner, shifted, phasor, table, up, low):
    shape = up.shape[1:]
    waves = forward([(inner[s, 0], inner[s, 1]) for s in slots], table)
    hr, hi = phasor[0], phasor[1]
    waves = backward([(tr * hr + ti * hi, ti * hr - tr * hi) for tr, ti in waves], table)
    for s, (qr, qi) in zip(slots, waves):
        w = Window(info, tile, s, shape)
        pr, pi = shifted[tile, s, 0], shifted[tile, s, 1]
        w.deposit(up, low, 0, pr * qr + pi * qi)
        w.deposit(up, low, 1, pr * qi - pi * qr)


def own_kernel(
    info, own, east, south, corner, wave, amp, shifted, phasor, table, up2, low2, up1, low1, inner
):
    clear(up2, low2, up1, low1)
    quads = (own, east, south.at[2:4], corner)

    def body(slots):
        second_step(info, 0, slots, quads, wave, amp, table, inner, up2, low2)
        third_step(info, 0, slots, inner, shifted, phasor, table, up1, low1)

    each_group(info, 0, body)


def west_second_kernel(
    info, own, south, west, west_south, wave, amp, table, up_in, low_in, inner, up, low
):
    up[...] = up_in[...]
    low[...] = low_in[...]
    quads = (west, own, west_south, south.at[2:4])
    each_group(
        info, 1, lambda slots: second_step(info, 1, slots, quads, wave, amp, table, inner, up, low)
    )


def west_third_kernel(info, inner, shifted, phasor, table, up_in, low_in, up, low):
    up[...] = up_in[...]
    low[...] = low_in[...]
    each_group(
        info, 1, lambda slots: third_step(info, 1, slots, inner, shifted, phasor, table, up, low)
    )


def update_kernel(info, planes, up, moved, power_up, power_moved, *refs):
    out = refs[-1]
    out[...] = planes[...] + (up[...] + moved[...]) / (power_up[...] + power_moved[...] + 1.0)


def update(info, planes, up, moved, power_up, power_moved, which, at, before=None):
    block = (1,) + planes.shape[1:]
    shape = (2 * planes.shape[0],) + planes.shape[1:]
    each = pl.BlockSpec(block, lambda i: (i, 0, 0))
    weight = pl.BlockSpec(block, lambda i: (which, 0, 0))
    operands = [info, planes, up, moved, power_up, power_moved]
    in_specs = [SMEM, each, each, each, weight, weight]
    aliases = {}
    if before is not None:
        aliases = {len(operands): 0}
        operands.append(before)
        in_specs.append(pl.BlockSpec(memory_space=pl.ANY))
    return pl.pallas_call(
        update_kernel,
        grid=(planes.shape[0],),
        out_shape=pltpu.HBM(shape, F32),
        in_specs=in_specs,
        out_specs=pl.BlockSpec(block, lambda i: (i + at, 0, 0)),
        input_output_aliases=aliases,
        compiler_params=pltpu.CompilerParams(vmem_limit_bytes=8 << 20),
        cost_estimate=pl.CostEstimate(flops=10**6, bytes_accessed=10**3, transcendentals=0),
    )(*operands)


def call(kernel, shapes, *operands, scratch=(), microseconds=COST):
    return pl.pallas_call(
        kernel,
        out_shape=[pltpu.VMEM(s, F32) for s in shapes],
        in_specs=[SMEM] + [VMEM] * (len(operands) - 1),
        out_specs=[VMEM] * len(shapes),
        scratch_shapes=[pltpu.VMEM(s, F32) for s in scratch],
        compiler_params=pltpu.CompilerParams(vmem_limit_bytes=20 << 20),
        cost_estimate=pl.CostEstimate(
            flops=int(microseconds * 10**9), bytes_accessed=int(microseconds * 10**6), transcendentals=0
        ),
    )(*operands)


def on_device(object_planes, probe, phase, coords, live, amplitude):
    width = probe.shape[-1]
    slots = coords.shape[2]
    tile = (width, width)
    pair = (2,) + tile
    table = jnp.asarray(transform_tables(width))
    order = jnp.asarray(order_table(width))

    own_info = jnp.concatenate([coords.reshape(1, 2 * slots), live.reshape(1, 1)], axis=1)
    first, second = object_planes[0:2], object_planes[2:4]
    info = jnp.concatenate([own_info, from_behind(own_info, "tx", 1)])
    east1 = from_behind(first, "tx", -1)
    west1 = from_behind(first, "tx", 1)
    east2 = from_behind(second, "tx", -1)
    west2 = from_behind(second, "tx", 1)
    south = from_behind(object_planes, "ty", -1)
    phasor = jnp.stack([jnp.cos(phase), jnp.sin(phase)])
    amp, phasor = call(prep_kernel, [(slots,) + tile, pair], own_info, amplitude[0, 0], phasor, order)
    amp_west = from_behind(amp, "tx", 1)
    shifted = call(shift_kernel, [(2, slots) + pair], info, probe)[0]

    east1, west1, amp, phasor, shifted, table = lax.optimization_barrier(
        (east1, west1, amp, phasor, shifted, table)
    )
    corner1 = from_behind(east1, "ty", -1)
    west_south1 = from_behind(west1, "ty", -1)
    east2, west2 = lax.optimization_barrier((east2, west2))
    corner2 = from_behind(east2, "ty", -1)
    west_south2 = from_behind(west2, "ty", -1)
    wave, power_up, power_low = call(
        first_kernel,
        [(2, slots) + pair, pair, pair],
        info, first, east1, south, corner1, west1, west_south1, shifted, phasor, table,
        microseconds=COST_BIG,
    )
    power_moved = from_behind(power_low, "ty", 1)
    corner2, west_south2 = lax.optimization_barrier((corner2, west_south2))
    up2, low2, up1, low1 = call(
        own_kernel,
        [pair] * 4,
        info, second, east2, south, corner2, wave, amp, shifted, phasor, table,
        scratch=[(slots,) + pair], microseconds=COST_BIG,
    )
    amp_west, power_moved = lax.optimization_barrier((amp_west, power_moved))
    inner, up2, low2 = call(
        west_second_kernel,
        [(slots,) + pair, pair, pair],
        info, second, south, west2, west_south2, wave, amp_west, table, up2, low2,
    )
    moved2 = from_behind(low2, "ty", 1)
    up1, low1 = call(
        west_third_kernel, [pair, pair], info, inner, shifted, phasor, table, up1, low1
    )
    moved1 = from_behind(low1, "ty", 1)
    out = update(own_info, second, up2, moved2, power_up, power_moved, 0, 2)
    return update(own_info, first, up1, moved1, power_up, power_moved, 1, 0, out)


def solution(mesh):
    return jax.shard_map(
        on_device,
        mesh=mesh,
        in_specs=(
            P(None, ("groups", "ty"), "tx"),
            P(),
            P(),
            P(("groups", "ty"), "tx", None, None),
            P(("groups", "ty"), "tx"),
            P(("groups", "ty"), "tx", None, None, None),
        ),
        out_specs=P(None, ("groups", "ty"), "tx"),
        check_vma=False,
    )
```

```python
import functools
import math

import jax
import jax.numpy as jnp
import ml_dtypes
import numpy as np
from jax import lax
from jax.experimental import pallas as pl
from jax.experimental.pallas import tpu as pltpu
from jax.sharding import PartitionSpec as P

F32 = jnp.float32
BF16 = jnp.bfloat16
VMEM = pl.BlockSpec(memory_space=pltpu.VMEM)
NOTE_ROWS = 8
SMEM = pl.BlockSpec(memory_space=pltpu.SMEM)


def from_behind(block, axis, distance):
    devices = range(lax.axis_size(axis))
    route = [(i - distance, i) for i in devices if i - distance in devices]
    return lax.ppermute(block, axis, route)


def transform_tables(width):
    half = width // 2
    n = np.arange(half)[:, None]
    k = np.arange(half)[None, :]
    out = []
    for odd in (0, 1):
        angle = -2.0 * math.pi * ((n * (2 * k + odd)) % width) / width
        wr, wi = np.cos(angle) / math.sqrt(width), np.sin(angle) / math.sqrt(width)
        real = np.block([[wr, wi], [-wi, wr]])
        head = real.astype(ml_dtypes.bfloat16)
        tail = (real - head.astype(np.float64)).astype(ml_dtypes.bfloat16)
        out += [head, tail]
    out += [np.ascontiguousarray(m.T) for m in out]
    return np.stack(out)


def order_table(width):
    half = width // 2
    table = np.zeros((2, width, width), ml_dtypes.bfloat16)
    source = np.concatenate([np.arange(0, width, 2), np.arange(1, width, 2)])
    table[0, np.arange(width), source] = 1.0
    table[1] = table[0].T
    return table


def split(x):
    head = x.astype(BF16)
    return head, (x - head.astype(F32)).astype(BF16)


def mm(a, b):
    return jnp.dot(a, b, preferred_element_type=F32)


def right_mul(x, table, at):
    head, tail = split(x)
    return mm(head, table[at]) + mm(tail, table[at]) + mm(head, table[at + 1])


def left_mul(x, table, at):
    head, tail = split(x)
    return mm(table[at], head) + mm(table[at], tail) + mm(table[at + 1], head)


def stack_rows(blocks):
    return jnp.concatenate(blocks, axis=0)


def stack_cols(blocks):
    return jnp.concatenate(blocks, axis=1)


def forward(waves, table):
    half = waves[0][0].shape[0] // 2
    steps = []
    for xr, xi in waves:
        sums = stack_rows([xr[:half] + xr[half:], xi[:half] + xi[half:]])
        diffs = stack_rows([xr[:half] - xr[half:], xi[:half] - xi[half:]])
        steps.append((left_mul(sums, table, 4), left_mul(diffs, table, 6)))
    out = []
    for even, odd in steps:
        yr = stack_rows([even[:half], odd[:half]])
        yi = stack_rows([even[half:], odd[half:]])
        sums = stack_cols([yr[:, :half] + yr[:, half:], yi[:, :half] + yi[:, half:]])
        diffs = stack_cols([yr[:, :half] - yr[:, half:], yi[:, :half] - yi[:, half:]])
        out.append((right_mul(sums, table, 0), right_mul(diffs, table, 2)))
    return [
        (stack_cols([even[:, :half], odd[:, :half]]), stack_cols([even[:, half:], odd[:, half:]]))
        for even, odd in out
    ]


def backward(waves, table):
    half = waves[0][0].shape[0] // 2
    steps = []
    for xr, xi in waves:
        even = left_mul(stack_rows([xr[:half], xi[:half]]), table, 0)
        odd = left_mul(stack_rows([xr[half:], xi[half:]]), table, 2)
        steps.append((even, odd))
    out = []
    for even, odd in steps:
        yr = stack_rows([even[:half] + odd[:half], even[:half] - odd[:half]])
        yi = stack_rows([even[half:] + odd[half:], even[half:] - odd[half:]])
        even = right_mul(stack_cols([yr[:, :half], yi[:, :half]]), table, 4)
        odd = right_mul(stack_cols([yr[:, half:], yi[:, half:]]), table, 6)
        out.append((even, odd))
    return [
        tuple(
            stack_cols([even[:, part] + odd[:, part], even[:, part] - odd[:, part]])
            for part in (slice(0, half), slice(half, None))
        )
        for even, odd in out
    ]


class Window:
    def __init__(self, info, tile, slot, shape):
        slots = (info.shape[1] - 1) // 2
        rows = lax.broadcasted_iota(jnp.int32, shape, 0)
        cols = lax.broadcasted_iota(jnp.int32, shape, 1)
        self.low = rows < info[tile, 2 * slot]
        self.right = cols < info[tile, 2 * slot + 1]
        mine = self.right if tile else ~self.right
        mine = mine & (slot < info[tile, 2 * slots])
        self.keep_up = mine & ~self.low
        self.keep_low = mine & self.low

    def pick(self, quads, plane):
        own, east, south, corner = (q[plane, 0 : self.low.shape[0]] for q in quads)
        return jnp.where(self.low, jnp.where(self.right, corner, south), jnp.where(self.right, east, own))

    def deposit(self, up, low, plane, value):
        up[plane] += jnp.where(self.keep_up, value, 0.0)
        low[plane] += jnp.where(self.keep_low, value, 0.0)


def each_group(info, tile, body):
    slots = (info.shape[1] - 1) // 2
    group = 2 if slots % 2 == 0 else 1

    def step(g, carry):
        body([g * group + j for j in range(group)])
        return carry

    lax.fori_loop(0, (info[tile, 2 * slots] + group - 1) // group, step, 0)


def clear(*refs):
    for ref in refs:
        ref[...] = jnp.zeros_like(ref)


def shift_probe(info, tile, probe, shifted, up, low):
    slots = shifted.shape[0]

    def body(s, carry):
        top, left = info[tile, 2 * s], info[tile, 2 * s + 1]
        moved = [pltpu.roll(pltpu.roll(probe[part], top, 0), left, 1) for part in range(2)]
        for part in range(2):
            shifted[s, part] = moved[part]
        window = Window(info, tile, s, probe.shape[1:])
        window.deposit(up, low, 0, moved[0] * moved[0] + moved[1] * moved[1])
        return carry

    lax.fori_loop(0, info[tile, 2 * slots], body, 0)


def own_prep_kernel(coords, live, probe, amp, phasor, order, shifted, amp_out, phasor_out, up, low, info):
    slots = amp.shape[0]
    clear(up, low)
    for s in range(slots):
        for axis in range(2):
            info[0, 2 * s + axis] = coords[0, 0, axis, s]
    info[0, 2 * slots] = live[0, 0]

    def reorder(x):
        head, tail = split(x)
        once = mm(head, order[1]) + mm(tail, order[1])
        head, tail = split(once)
        return mm(order[0], head) + mm(order[0], tail)

    for part in range(2):
        phasor_out[part] = reorder(phasor[part])

    def reorder_amp(s, carry):
        amp_out[s] = reorder(amp[s])
        return carry

    lax.fori_loop(0, live[0, 0], reorder_amp, 0)
    shift_probe(info, 0, probe, shifted, up, low)


def west_prep_kernel(coords, live, probe, west, up_in, low_in, shifted, up, low, info, note, sem):
    up[...] = up_in[...]
    low[...] = low_in[...]
    copy = pltpu.make_async_copy(west.at[0, probe.shape[1] :, 0 : note.shape[1]], note, sem)
    copy.start()
    copy.wait()
    slots = shifted.shape[0]
    for s in range(slots):
        for axis in range(2):
            info[0, 2 * s + axis] = coords[0, 0, axis, s]
            info[1, 2 * s + axis] = note[0, 2 * s + axis].astype(jnp.int32)
    info[0, 2 * slots] = live[0, 0]
    info[1, 2 * slots] = note[0, 2 * slots].astype(jnp.int32)
    shift_probe(info, 1, probe, shifted, up, low)


def first_step(info, tile, slots, quads, shifted, phasor, table, wave, up, low):
    shape = up.shape[1:]
    windows = [Window(info, tile, s, shape) for s in slots]
    waves = []
    for s, w in zip(slots, windows):
        fr, fi = w.pick(quads, 0), w.pick(quads, 1)
        pr, pi = shifted[s, 0], shifted[s, 1]
        waves.append((pr * fr - pi * fi, pr * fi + pi * fr))
    waves = forward(waves, table)
    hr, hi = phasor[0], phasor[1]
    waves = backward([(ur * hr - ui * hi, ur * hi + ui * hr) for ur, ui in waves], table)
    for s, w, (wr, wi) in zip(slots, windows, waves):
        wave[s, 0] = wr
        wave[s, 1] = wi
        w.deposit(up, low, 0, wr * wr + wi * wi)


def own_first_kernel(
    info, own, east, south, corner, shifted, phasor, table, up_in, low_in, wave, up, low
):
    up[0] = jnp.zeros_like(up[0])
    low[0] = jnp.zeros_like(low[0])
    up[1] = up_in[0]
    low[1] = low_in[0]
    quads = (own, east, south.at[0:2], corner)
    each_group(
        info, 0, lambda s: first_step(info, 0, s, quads, shifted, phasor, table, wave, up, low)
    )


def west_first_kernel(
    info, own, south, west, west_south, shifted, phasor, table, up_in, low_in, wave, up, low
):
    up[...] = up_in[...]
    low[...] = low_in[...]
    quads = (west, own, west_south, south.at[0:2])
    each_group(
        info, 1, lambda s: first_step(info, 1, s, quads, shifted, phasor, table, wave, up, low)
    )


def second_step(info, tile, slots, quads, wave, amp, table, inner, up, low):
    shape = up.shape[1:]
    windows = [Window(info, tile, s, shape) for s in slots]
    waves = []
    for s, w in zip(slots, windows):
        sr, si = w.pick(quads, 0), w.pick(quads, 1)
        wr, wi = wave[s, 0], wave[s, 1]
        waves.append((wr * sr - wi * si, wr * si + wi * sr))
    scaled = []
    for s, (fr, fi) in zip(slots, forward(waves, table)):
        ratio = amp[s] * lax.rsqrt(jnp.maximum(fr * fr + fi * fi, 0.25)) - 1.0
        scaled.append((fr * ratio, fi * ratio))
    for s, w, (br, bi) in zip(slots, windows, backward(scaled, table)):
        sr, si = w.pick(quads, 0), w.pick(quads, 1)
        wr, wi = wave[s, 0], wave[s, 1]
        inner[s, 0] = sr * br + si * bi
        inner[s, 1] = sr * bi - si * br
        w.deposit(up, low, 0, wr * br + wi * bi)
        w.deposit(up, low, 1, wr * bi - wi * br)


def third_step(info, tile, slots, inner, shifted, phasor, table, up, low):
    shape = up.shape[1:]
    waves = forward([(inner[s, 0], inner[s, 1]) for s in slots], table)
    hr, hi = phasor[0], phasor[1]
    waves = backward([(tr * hr + ti * hi, ti * hr - tr * hi) for tr, ti in waves], table)
    for s, (qr, qi) in zip(slots, waves):
        w = Window(info, tile, s, shape)
        pr, pi = shifted[s, 0], shifted[s, 1]
        w.deposit(up, low, 0, pr * qr + pi * qi)
        w.deposit(up, low, 1, pr * qi - pi * qr)


def own_kernel(
    info, own, east, south, corner, wave, amp, shifted, phasor, table, up2, low2, up1, low1, inner
):
    clear(up2, low2, up1, low1)
    quads = (own, east, south.at[2:4], corner)

    def body(slots):
        second_step(info, 0, slots, quads, wave, amp, table, inner, up2, low2)
        third_step(info, 0, slots, inner, shifted, phasor, table, up1, low1)

    each_group(info, 0, body)


def west_second_kernel(
    info, own, south, west, west_south, wave, amp, table, up_in, low_in, inner, up, low
):
    up[...] = up_in[...]
    low[...] = low_in[...]
    quads = (west, own, west_south, south.at[2:4])
    each_group(
        info, 1, lambda slots: second_step(info, 1, slots, quads, wave, amp, table, inner, up, low)
    )


def west_third_kernel(info, inner, shifted, phasor, table, up_in, low_in, up, low):
    up[...] = up_in[...]
    low[...] = low_in[...]
    each_group(
        info, 1, lambda slots: third_step(info, 1, slots, inner, shifted, phasor, table, up, low)
    )


def load_kernel(coords, live, source, out, sem, at):
    count, _, width = out.shape
    rows = source.shape[1]
    copy = pltpu.make_async_copy(source.at[at : at + count], out.at[:, 0:rows], sem)
    copy.start()
    slots = coords.shape[-1]
    lane = lax.broadcasted_iota(jnp.int32, (NOTE_ROWS, width), 1)
    note = jnp.where(lane == 2 * slots, live[0, 0], 0)
    for s in range(slots):
        for axis in range(2):
            note = jnp.where(lane == 2 * s + axis, coords[0, 0, axis, s], note)
    out[0, rows:] = note.astype(F32)
    for plane in range(1, count):
        out[plane, rows:] = jnp.zeros((NOTE_ROWS, width), F32)
    copy.wait()


def load(coords, live, source, at, count):
    return pl.pallas_call(
        functools.partial(load_kernel, at=at),
        out_shape=pltpu.VMEM((count, source.shape[1] + NOTE_ROWS, source.shape[2]), source.dtype),
        in_specs=[SMEM, SMEM, pl.BlockSpec(memory_space=pl.ANY)],
        out_specs=VMEM,
        scratch_shapes=[pltpu.SemaphoreType.DMA],
        compiler_params=pltpu.CompilerParams(vmem_limit_bytes=4 << 20),
        cost_estimate=pl.CostEstimate(flops=10**6, bytes_accessed=10**3, transcendentals=0),
    )(coords, live, source)


def update_kernel(planes, up, moved, power_up, power_moved, *refs, which, at):
    out, result, sems = refs[-3:]
    weight = 1.0 / (power_up[which] + power_moved[which] + 1.0)
    copies = []
    for part in range(planes.shape[0]):
        result[part] = planes[part, 0 : up.shape[1]] + (up[part] + moved[part]) * weight
        copies.append(pltpu.make_async_copy(result.at[part], out.at[at + part], sems.at[part]))
        copies[-1].start()
    for copy in copies:
        copy.wait()


def update(planes, up, moved, power_up, power_moved, which, at, before=None):
    shape = (2 * planes.shape[0],) + up.shape[1:]
    operands = [planes, up, moved, power_up, power_moved]
    in_specs = [VMEM] * len(operands)
    aliases = {}
    if before is not None:
        aliases = {len(operands): 0}
        operands.append(before)
        in_specs.append(pl.BlockSpec(memory_space=pl.ANY))
    return pl.pallas_call(
        functools.partial(update_kernel, which=which, at=at),
        out_shape=pltpu.HBM(shape, F32),
        in_specs=in_specs,
        out_specs=pl.BlockSpec(memory_space=pl.ANY),
        input_output_aliases=aliases,
        scratch_shapes=[pltpu.VMEM(up.shape, F32), pltpu.SemaphoreType.DMA((planes.shape[0],))],
        compiler_params=pltpu.CompilerParams(vmem_limit_bytes=4 << 20),
        cost_estimate=pl.CostEstimate(flops=10**6, bytes_accessed=10**3, transcendentals=0),
    )(*operands)


def call(kernel, shapes, *operands, scalars=1, scratch=(), info_shape=None):
    outs, out_specs = [pltpu.VMEM(s, F32) for s in shapes], [VMEM] * len(shapes)
    if info_shape is not None:
        outs.append(jax.ShapeDtypeStruct(info_shape, jnp.int32))
        out_specs.append(SMEM)
    return pl.pallas_call(
        kernel,
        out_shape=outs,
        in_specs=[SMEM] * scalars + [VMEM] * (len(operands) - scalars),
        out_specs=out_specs,
        scratch_shapes=scratch,
        compiler_params=pltpu.CompilerParams(vmem_limit_bytes=20 << 20),
        cost_estimate=pl.CostEstimate(flops=10**6, bytes_accessed=10**3, transcendentals=0),
    )(*operands)


def on_device(object_planes, probe, phase, coords, live, amplitude):
    width = probe.shape[-1]
    slots = coords.shape[2]
    tile = (width, width)
    pair = (2,) + tile
    table = jnp.asarray(transform_tables(width))
    order = jnp.asarray(order_table(width))

    coords = jnp.swapaxes(coords, 2, 3)
    first = load(coords, live, object_planes, 0, 2)
    west1 = from_behind(first, "tx", 1)
    east1 = from_behind(first, "tx", -1)
    south = from_behind(object_planes, "ty", -1)
    second = load(coords, live, object_planes, 2, 2)
    west2 = from_behind(second, "tx", 1)
    east2 = from_behind(second, "tx", -1)
    phasor = jnp.stack([jnp.cos(phase), jnp.sin(phase)])
    shifted, amp, phasor, cover_up, cover_low, _ = call(
        own_prep_kernel,
        [(slots,) + pair, (slots,) + tile, pair, (1,) + tile, (1,) + tile],
        coords, live, probe, amplitude[0, 0], phasor, order,
        scalars=2, info_shape=(1, 2 * slots + 1),
    )
    amp_west = from_behind(amp, "tx", 1)

    east1, west1, amp, phasor, shifted, table = lax.optimization_barrier(
        (east1, west1, amp, phasor, shifted, table)
    )
    corner1 = from_behind(east1, "ty", -1)
    west_south1 = from_behind(west1, "ty", -1)
    west_shifted, cover_up, cover_low, info = call(
        west_prep_kernel,
        [(slots,) + pair, (1,) + tile, (1,) + tile],
        coords, live, probe, west1, cover_up, cover_low,
        scalars=2, info_shape=(2, 2 * slots + 1),
        scratch=[pltpu.SMEM((NOTE_ROWS, 128), F32), pltpu.SemaphoreType.DMA],
    )
    east2, west2, west_shifted = lax.optimization_barrier((east2, west2, west_shifted))
    corner2 = from_behind(east2, "ty", -1)
    west_south2 = from_behind(west2, "ty", -1)
    corner1, east2, west2 = lax.optimization_barrier((corner1, east2, west2))
    wave_shape = (slots,) + pair
    wave, power_up, power_low = call(
        own_first_kernel,
        [wave_shape, pair, pair],
        info, first, east1, south, corner1, shifted, phasor, table, cover_up, cover_low,
    )
    west_wave, power_up, power_low = call(
        west_first_kernel,
        [wave_shape, pair, pair],
        info, first, south, west1, west_south1, west_shifted, phasor, table, power_up, power_low,
    )
    power_moved = from_behind(power_low, "ty", 1)
    corner2, west_south2 = lax.optimization_barrier((corner2, west_south2))
    up2, low2, up1, low1 = call(
        own_kernel,
        [pair] * 4,
        info, second, east2, south, corner2, wave, amp, shifted, phasor, table,
        scratch=[pltpu.VMEM(wave_shape, F32)],
    )
    amp_west, power_moved = lax.optimization_barrier((amp_west, power_moved))
    inner, up2, low2 = call(
        west_second_kernel,
        [wave_shape, pair, pair],
        info, second, south, west2, west_south2, west_wave, amp_west, table, up2, low2,
    )
    moved2 = from_behind(low2, "ty", 1)
    up1, low1 = call(
        west_third_kernel, [pair, pair], info, inner, west_shifted, phasor, table, up1, low1
    )
    moved1 = from_behind(low1, "ty", 1)
    out = update(second, up2, moved2, power_up, power_moved, 0, 2)
    return update(first, up1, moved1, power_up, power_moved, 1, 0, out)


def solution(mesh):
    return jax.shard_map(
        on_device,
        mesh=mesh,
        in_specs=(
            P(None, ("groups", "ty"), "tx"),
            P(),
            P(),
            P(("groups", "ty"), "tx", None, None),
            P(("groups", "ty"), "tx"),
            P(("groups", "ty"), "tx", None, None, None),
        ),
        out_specs=P(None, ("groups", "ty"), "tx"),
        check_vma=False,
    )
```

```python
import functools
import math

import jax
import jax.numpy as jnp
import ml_dtypes
import numpy as np
from jax import lax
from jax.experimental import pallas as pl
from jax.experimental.pallas import tpu as pltpu
from jax.sharding import PartitionSpec as P

F32 = jnp.float32
BF16 = jnp.bfloat16
VMEM = pl.BlockSpec(memory_space=pltpu.VMEM)
NOTE_ROWS = 8
SMEM = pl.BlockSpec(memory_space=pltpu.SMEM)


def from_behind(block, axis, distance):
    devices = range(lax.axis_size(axis))
    route = [(i - distance, i) for i in devices if i - distance in devices]
    return lax.ppermute(block, axis, route)


def true_index(position, width):
    return jnp.where(position < width // 2, position, width + width // 2 - 1 - position)


def transform_tables(width):
    half = width // 2
    index = 2 * np.arange(half) + 1
    angle = 2.0 * math.pi * ((index[:, None] * index[None, :]) % (4 * width)) / (4 * width)
    out = []
    for real in (np.cos(angle), np.sin(angle)):
        real = real / math.sqrt(width)
        head = real.astype(ml_dtypes.bfloat16)
        tail = (real - head.astype(np.float64)).astype(ml_dtypes.bfloat16)
        out.append(np.block([[head, tail], [head, tail]]))
    out += [np.ascontiguousarray(m.T) for m in out]
    return np.stack(out)


def fold_index(width):
    return np.concatenate([np.arange(width // 2), np.arange(width // 2, width)[::-1]])


def order_matrix(width):
    rows = lax.broadcasted_iota(jnp.int32, (width, width), 0)
    cols = lax.broadcasted_iota(jnp.int32, (width, width), 1)
    return jnp.where(true_index(rows, width) == cols, 1.0, 0.0).astype(BF16)


def ramp_table(width):
    where = fold_index(width)
    angle = math.pi * (where[:, None] + where[None, :]) / width
    return np.stack([np.cos(angle), np.sin(angle)]).astype(np.float32)


def split(x):
    head = x.astype(BF16)
    return head, (x - head.astype(F32)).astype(BF16)


def mm(a, b):
    return jnp.dot(a, b, preferred_element_type=F32)


def reorder(x, order):
    head, tail = (mm(piece, order).astype(BF16) for piece in split(x))
    return mm(order, head) + mm(order, tail)


def stack_rows(blocks):
    return jnp.concatenate(blocks, axis=0)


def stack_cols(blocks):
    return jnp.concatenate(blocks, axis=1)


def left_mul(x, table):
    half = x.shape[0]
    out = mm(table, stack_rows(split(x)))
    return out[:half] + out[half:]


def right_mul(x, table):
    half = x.shape[1]
    out = mm(stack_cols(split(x)), table)
    return out[:, :half] + out[:, half:]


def halves(x, axis):
    half = x.shape[axis] // 2
    return (x[:half], x[half:]) if axis == 0 else (x[:, :half], x[:, half:])


def one_side(waves, table, axis, sign):
    mul, stack = (left_mul, stack_rows) if axis == 0 else (right_mul, stack_cols)
    cos_table, sin_table = (table[2], table[3]) if axis == 0 else (table[0], table[1])
    parts = []
    for wave in waves:
        cos_part, sin_part = [], []
        for x in wave:
            a, b = halves(x, axis)
            cos_part.append(mul(a - b, cos_table))
            sin_part.append(mul(a + b, sin_table))
        parts.append((cos_part, sin_part))
    out = []
    for (cr, ci), (sr, si) in parts:
        if sign > 0:
            out.append((stack([si + cr, si - cr]), stack([ci - sr, -ci - sr])))
        else:
            out.append((stack([cr - si, -cr - si]), stack([sr + ci, sr - ci])))
    return out


def forward(waves, table):
    return one_side(one_side(waves, table, 0, 1), table, 1, 1)


def backward(waves, table):
    return one_side(one_side(waves, table, 0, -1), table, 1, -1)


class Window:
    def __init__(self, info, tile, slot, shape):
        slots = (info.shape[1] - 1) // 2
        rows = true_index(lax.broadcasted_iota(jnp.int32, shape, 0), shape[0])
        cols = true_index(lax.broadcasted_iota(jnp.int32, shape, 1), shape[1])
        is_live = slot < info[tile, 2 * slots]
        left = jnp.where(is_live, info[tile, 2 * slot + 1], 0 if tile else shape[1])
        self.low = rows < info[tile, 2 * slot]
        self.right = cols < left
        mine = self.right if tile else ~self.right
        self.keep_up = mine & ~self.low
        self.keep_low = mine & self.low

    def pick(self, quads, plane):
        own, east, south, corner = (q[plane, 0 : self.low.shape[0]] for q in quads)
        return jnp.where(self.low, jnp.where(self.right, corner, south), jnp.where(self.right, east, own))


def deposit(up, low, plane, windows, values):
    up[plane] += sum(jnp.where(w.keep_up, v, 0.0) for w, v in zip(windows, values))
    low[plane] += sum(jnp.where(w.keep_low, v, 0.0) for w, v in zip(windows, values))


def each_group(info, tile, body):
    slots = (info.shape[1] - 1) // 2
    group = 2 if slots % 2 == 0 else 1

    def step(g, carry):
        body([g * group + j for j in range(group)])
        return carry

    lax.fori_loop(0, (info[tile, 2 * slots] + group - 1) // group, step, 0)


def clear(*refs):
    for ref in refs:
        ref[...] = jnp.zeros_like(ref)


def shift_probe(info, tile, probe, ramp, shifted, up, low):
    shape = probe.shape[1:]
    rows = lax.broadcasted_iota(jnp.int32, shape, 0)
    cols = lax.broadcasted_iota(jnp.int32, shape, 1)

    def moved(position, source, offset):
        wanted = true_index(position, shape[0]) - offset
        wanted = jnp.where(wanted < 0, wanted + shape[0], wanted)
        return jnp.where(wanted == source, 1.0, 0.0).astype(BF16)

    def body(slots):
        windows, powers = [Window(info, tile, s, shape) for s in slots], []
        pieces = [split(probe[part]) for part in range(2)]
        for s in slots:
            to_cols = moved(cols, rows, info[tile, 2 * s + 1])
            to_rows = moved(rows, cols, info[tile, 2 * s])
            once = [[mm(piece, to_cols).astype(BF16) for piece in both] for both in pieces]
            pr, pi = (mm(to_rows, head) + mm(to_rows, tail) for head, tail in once)
            shifted[s, 0] = pr * ramp[0] - pi * ramp[1]
            shifted[s, 1] = pr * ramp[1] + pi * ramp[0]
            powers.append(pr * pr + pi * pi)
        deposit(up, low, 0, windows, powers)

    each_group(info, tile, body)


def own_prep_kernel(
    coords, live, probe, amp, phasor, ramp, shifted, amp_out, phasor_out, up, low, info
):
    slots = amp.shape[0]
    for s in range(slots):
        for axis in range(2):
            info[0, 2 * s + axis] = coords[0, 0, axis, s]
    info[0, 2 * slots] = live[0, 0]
    clear(up, low)
    order = order_matrix(amp.shape[1])
    for part in range(2):
        phasor_out[part] = reorder(phasor[part], order)
    for s in range(slots):
        amp_out[s] = reorder(amp[s], order)
    shift_probe(info, 0, probe, ramp, shifted, up, low)


def west_prep_kernel(coords, live, probe, ramp, west, up_in, low_in, up, low, shifted, info, note, sem):
    copy = pltpu.make_async_copy(west.at[0, probe.shape[1] :, 0 : note.shape[1]], note, sem)
    copy.start()
    copy.wait()
    slots = shifted.shape[0]
    for s in range(slots):
        for axis in range(2):
            info[0, 2 * s + axis] = coords[0, 0, axis, s]
            info[1, 2 * s + axis] = note[0, 2 * s + axis].astype(jnp.int32)
    info[0, 2 * slots] = live[0, 0]
    info[1, 2 * slots] = note[0, 2 * slots].astype(jnp.int32)
    shift_probe(info, 1, probe, ramp, shifted, up, low)


def first_step(info, tile, slots, quads, shifted, phasor, table, wave, up, low):
    shape = up.shape[1:]
    windows = [Window(info, tile, s, shape) for s in slots]
    waves = []
    for s, w in zip(slots, windows):
        fr, fi = w.pick(quads, 0), w.pick(quads, 1)
        pr, pi = shifted[s, 0], shifted[s, 1]
        waves.append((pr * fr - pi * fi, pr * fi + pi * fr))
    waves = forward(waves, table)
    hr, hi = phasor[0], phasor[1]
    waves = backward([(ur * hr - ui * hi, ur * hi + ui * hr) for ur, ui in waves], table)
    for s, (wr, wi) in zip(slots, waves):
        wave[s, 0] = wr
        wave[s, 1] = wi
    deposit(up, low, 0, windows, [wr * wr + wi * wi for wr, wi in waves])


def first_kernel(
    info, own, east, south, corner, west, west_south, shifted, west_shifted, phasor, table,
    cover_up, cover_low, wave, west_wave, up, low,
):
    up[0] = jnp.zeros_like(up[0])
    low[0] = jnp.zeros_like(low[0])
    up[1] = cover_up[0]
    low[1] = cover_low[0]
    quads = (own, east, south.at[0:2], corner)
    each_group(
        info, 0, lambda s: first_step(info, 0, s, quads, shifted, phasor, table, wave, up, low)
    )
    west_quads = (west, own, west_south, south.at[0:2])
    each_group(
        info,
        1,
        lambda s: first_step(
            info, 1, s, west_quads, west_shifted, phasor, table, west_wave, up, low
        ),
    )


def second_step(info, tile, slots, quads, wave, amp, table, inner, up, low, picked):
    windows = [Window(info, tile, s, up.shape[1:]) for s in slots]
    waves = []
    for j, (s, w) in enumerate(zip(slots, windows)):
        sr, si = w.pick(quads, 0), w.pick(quads, 1)
        picked[j, 0] = sr
        picked[j, 1] = si
        wr, wi = wave[s, 0], wave[s, 1]
        waves.append((wr * sr - wi * si, wr * si + wi * sr))
    scaled = []
    for s, (fr, fi) in zip(slots, forward(waves, table)):
        ratio = amp[s] * lax.rsqrt(jnp.maximum(fr * fr + fi * fi, 0.25)) - 1.0
        scaled.append((fr * ratio, fi * ratio))
    real, imag = [], []
    for j, (s, (br, bi)) in enumerate(zip(slots, backward(scaled, table))):
        sr, si = picked[j, 0], picked[j, 1]
        inner[s, 0] = sr * br + si * bi
        inner[s, 1] = sr * bi - si * br
        wr, wi = wave[s, 0], wave[s, 1]
        real.append(wr * br + wi * bi)
        imag.append(wr * bi - wi * br)
    deposit(up, low, 0, windows, real)
    deposit(up, low, 1, windows, imag)


def third_step(info, tile, slots, inner, shifted, phasor, table, up, low):
    waves = forward([(inner[s, 0], inner[s, 1]) for s in slots], table)
    hr, hi = phasor[0], phasor[1]
    waves = backward([(tr * hr + ti * hi, ti * hr - tr * hi) for tr, ti in waves], table)
    windows = [Window(info, tile, s, up.shape[1:]) for s in slots]
    real, imag = [], []
    for s, (qr, qi) in zip(slots, waves):
        pr, pi = shifted[s, 0], shifted[s, 1]
        real.append(pr * qr + pi * qi)
        imag.append(pr * qi - pi * qr)
    deposit(up, low, 0, windows, real)
    deposit(up, low, 1, windows, imag)


def own_kernel(
    info, own, east, south, corner, wave, amp, shifted, phasor, table, up2, low2, up1, low1, inner, picked
):
    clear(up2, low2, up1, low1)
    quads = (own, east, south.at[2:4], corner)

    def body(slots):
        second_step(info, 0, slots, quads, wave, amp, table, inner, up2, low2, picked)
        third_step(info, 0, slots, inner, shifted, phasor, table, up1, low1)

    each_group(info, 0, body)


def west_second_kernel(
    info, own, south, west, west_south, wave, amp, table, up_in, low_in, up, low, inner, picked
):
    quads = (west, own, west_south, south.at[2:4])
    each_group(
        info,
        1,
        lambda slots: second_step(
            info, 1, slots, quads, wave, amp, table, inner, up, low, picked
        ),
    )


def west_third_kernel(info, inner, shifted, phasor, table, up_in, low_in, up, low):
    each_group(
        info, 1, lambda slots: third_step(info, 1, slots, inner, shifted, phasor, table, up, low)
    )


def load_first_kernel(source, raw, out, sem):
    load_planes(source, raw, (out,), sem, 0)


def load_second_kernel(coords, live, source, before, raw, out, whole, sem):
    count, rows, width = raw.shape
    slots = coords.shape[-1]
    lane = lax.broadcasted_iota(jnp.int32, (NOTE_ROWS, width), 1)
    note = jnp.where(lane == 2 * slots, live[0, 0], 0)
    for s in range(slots):
        for axis in range(2):
            note = jnp.where(lane == 2 * s + axis, coords[0, 0, axis, s], note)
    for plane in range(count):
        out[plane, rows:] = note.astype(F32)
    whole[0:count] = before[...]
    load_planes(source, raw, (out, whole.at[count:]), sem, count)


def load_planes(source, raw, outs, sem, at):
    count, rows, width = raw.shape
    copies = []
    for plane in range(count):
        copies.append(pltpu.make_async_copy(source.at[at + plane], raw.at[plane], sem.at[plane]))
        copies[-1].start()
    order = order_matrix(width)
    for plane in range(count):
        copies[plane].wait()
        ordered = reorder(raw[plane], order)
        for out in outs:
            out[plane, 0:rows] = ordered


def load(kernel, shapes, *operands, source):
    specs = [pl.BlockSpec(memory_space=pl.ANY) if k == source else SMEM if k < source else VMEM for k in range(len(operands))]
    operands = list(operands)
    operands[source] = pltpu.with_memory_space_constraint(operands[source], pltpu.HBM)
    return pl.pallas_call(
        kernel,
        out_shape=[pltpu.VMEM(s, F32) for s in shapes],
        in_specs=specs,
        out_specs=[VMEM] * len(shapes),
        scratch_shapes=[pltpu.SemaphoreType.DMA((shapes[0][0],))],
        compiler_params=pltpu.CompilerParams(vmem_limit_bytes=8 << 20),
        cost_estimate=pl.CostEstimate(flops=10**6, bytes_accessed=10**3, transcendentals=0),
    )(*operands)


def update_kernel(planes, up, moved, power_up, power_moved, *refs, which, at):
    out, result, sems = refs[-3:]
    weight = 1.0 / (power_up[which] + power_moved[which] + 1.0)
    order = order_matrix(weight.shape[0])
    copies = []
    for part in range(planes.shape[0]):
        result[part] = planes[part] + reorder((up[part] + moved[part]) * weight, order)
        copies.append(pltpu.make_async_copy(result.at[part], out.at[at + part], sems.at[part]))
        copies[-1].start()
    for copy in copies:
        copy.wait()


def update(planes, up, moved, power_up, power_moved, which, at, before=None):
    shape = (2 * planes.shape[0],) + up.shape[1:]
    operands = [planes, up, moved, power_up, power_moved]
    in_specs = [VMEM] * len(operands)
    aliases = {}
    if before is not None:
        aliases = {len(operands): 0}
        operands.append(before)
        in_specs.append(pl.BlockSpec(memory_space=pl.ANY))
    return pl.pallas_call(
        functools.partial(update_kernel, which=which, at=at),
        out_shape=pltpu.HBM(shape, F32),
        in_specs=in_specs,
        out_specs=pl.BlockSpec(memory_space=pl.ANY),
        input_output_aliases=aliases,
        scratch_shapes=[pltpu.VMEM(up.shape, F32), pltpu.SemaphoreType.DMA((planes.shape[0],))],
        compiler_params=pltpu.CompilerParams(vmem_limit_bytes=8 << 20),
        cost_estimate=pl.CostEstimate(flops=10**6, bytes_accessed=10**3, transcendentals=0),
    )(*operands)


def call(kernel, shapes, *operands, scalars=1, scratch=(), info_shape=None, add_to=0):
    outs, out_specs = [pltpu.VMEM(s, F32) for s in shapes], [VMEM] * len(shapes)
    if info_shape is not None:
        outs.append(jax.ShapeDtypeStruct(info_shape, jnp.int32))
        out_specs.append(SMEM)
    return pl.pallas_call(
        kernel,
        out_shape=outs,
        in_specs=[SMEM] * scalars + [VMEM] * (len(operands) - scalars),
        out_specs=out_specs,
        input_output_aliases={len(operands) - add_to + k: k for k in range(add_to)},
        scratch_shapes=scratch,
        compiler_params=pltpu.CompilerParams(vmem_limit_bytes=20 << 20),
        cost_estimate=pl.CostEstimate(flops=10**6, bytes_accessed=10**3, transcendentals=0),
    )(*operands)


def on_device(object_planes, probe, phase, coords, live, amplitude):
    width = probe.shape[-1]
    slots = coords.shape[2]
    tile = (width, width)
    pair = (2,) + tile
    one = (1,) + tile
    wave_shape = (slots,) + pair
    table = jnp.asarray(transform_tables(width))
    ramp = jnp.asarray(ramp_table(width))

    coords = jnp.swapaxes(coords, 2, 3)
    first_raw, first = load(load_first_kernel, [pair, pair], object_planes, source=0)
    west1 = from_behind(first, "tx", 1)
    east1 = from_behind(first, "tx", -1)
    second_raw, second, whole = load(
        load_second_kernel,
        [pair, (2, width + NOTE_ROWS, width), (4,) + tile],
        coords, live, object_planes, first, source=2,
    )
    west2 = from_behind(second, "tx", 1)
    east2 = from_behind(second, "tx", -1)
    south = from_behind(whole, "ty", -1)
    phasor = jnp.stack([jnp.cos(phase), jnp.sin(phase)])

    east1, west1, phasor, table = lax.optimization_barrier((east1, west1, phasor, table))
    corner1 = from_behind(east1, "ty", -1)
    west_south1 = from_behind(west1, "ty", -1)
    shifted, amp, phasor, cover_up, cover_low, _ = call(
        own_prep_kernel,
        [wave_shape, (slots,) + tile, pair, one, one],
        coords, live, probe, amplitude[0, 0], phasor, ramp,
        scalars=2, info_shape=(1, 2 * slots + 1),
    )
    amp_west = from_behind(amp, "tx", 1)
    east2, west2, shifted = lax.optimization_barrier((east2, west2, shifted))
    corner2 = from_behind(east2, "ty", -1)
    west_south2 = from_behind(west2, "ty", -1)
    west2, west_south1 = lax.optimization_barrier((west2, west_south1))
    cover_up, cover_low, west_shifted, info = call(
        west_prep_kernel,
        [one, one, wave_shape],
        coords, live, probe, ramp, west2, cover_up, cover_low,
        scalars=2, add_to=2, info_shape=(2, 2 * slots + 1),
        scratch=[pltpu.SMEM((NOTE_ROWS, 128), F32), pltpu.SemaphoreType.DMA],
    )
    wave, west_wave, power_up, power_low = call(
        first_kernel,
        [wave_shape, wave_shape, pair, pair],
        info, first, east1, south, corner1, west1, west_south1,
        shifted, west_shifted, phasor, table, cover_up, cover_low,
    )
    power_moved = from_behind(power_low, "ty", 1)
    corner2, west_south2 = lax.optimization_barrier((corner2, west_south2))
    up2, low2, up1, low1 = call(
        own_kernel,
        [pair] * 4,
        info, second, east2, south, corner2, wave, amp, shifted, phasor, table,
        scratch=[pltpu.VMEM(wave_shape, F32), pltpu.VMEM((2,) + pair, F32)],
    )
    amp_west, power_moved = lax.optimization_barrier((amp_west, power_moved))
    up2, low2, inner = call(
        west_second_kernel,
        [pair, pair, wave_shape],
        info, second, south, west2, west_south2, west_wave, amp_west, table, up2, low2,
        scratch=[pltpu.VMEM((2,) + pair, F32)], add_to=2,
    )
    moved2 = from_behind(low2, "ty", 1)
    up1, low1 = call(
        west_third_kernel,
        [pair, pair],
        info, inner, west_shifted, phasor, table, up1, low1,
        add_to=2,
    )
    moved1 = from_behind(low1, "ty", 1)
    out = update(second_raw, up2, moved2, power_up, power_moved, 0, 2)
    return update(first_raw, up1, moved1, power_up, power_moved, 1, 0, out)


def solution(mesh):
    return jax.shard_map(
        on_device,
        mesh=mesh,
        in_specs=(
            P(None, ("groups", "ty"), "tx"),
            P(),
            P(),
            P(("groups", "ty"), "tx", None, None),
            P(("groups", "ty"), "tx"),
            P(("groups", "ty"), "tx", None, None, None),
        ),
        out_specs=P(None, ("groups", "ty"), "tx"),
        check_vma=False,
    )
```

```python
import functools
import math

import jax
import jax.numpy as jnp
import ml_dtypes
import numpy as np
from jax import lax
from jax.experimental import pallas as pl
from jax.experimental.pallas import tpu as pltpu
from jax.sharding import PartitionSpec as P

F32 = jnp.float32
BF16 = jnp.bfloat16
VMEM = pl.BlockSpec(memory_space=pltpu.VMEM)
NOTE_ROWS = 8
SMEM = pl.BlockSpec(memory_space=pltpu.SMEM)


def from_behind(block, axis, distance):
    devices = range(lax.axis_size(axis))
    route = [(i - distance, i) for i in devices if i - distance in devices]
    return lax.ppermute(block, axis, route)


def true_index(position, width):
    return jnp.where(position < width // 2, position, width + width // 2 - 1 - position)


def transform_tables(width):
    half = width // 2
    index = 2 * np.arange(half) + 1
    angle = 2.0 * math.pi * ((index[:, None] * index[None, :]) % (4 * width)) / (4 * width)
    out = []
    for real in (np.cos(angle), np.sin(angle)):
        real = real / math.sqrt(width)
        head = real.astype(ml_dtypes.bfloat16)
        tail = (real - head.astype(np.float64)).astype(ml_dtypes.bfloat16)
        out.append(np.block([[head, tail], [head, tail]]))
    out += [np.ascontiguousarray(m.T) for m in out]
    return np.stack(out)


def fold_index(width):
    return np.concatenate([np.arange(width // 2), np.arange(width // 2, width)[::-1]])


def order_matrix(width):
    rows = lax.broadcasted_iota(jnp.int32, (width, width), 0)
    cols = lax.broadcasted_iota(jnp.int32, (width, width), 1)
    return jnp.where(true_index(rows, width) == cols, 1.0, 0.0).astype(BF16)


def ramp_table(width):
    where = fold_index(width)
    angle = math.pi * (where[:, None] + where[None, :]) / width
    return np.stack([np.cos(angle), np.sin(angle)]).astype(np.float32)


def split(x):
    head = x.astype(BF16)
    return head, (x - head.astype(F32)).astype(BF16)


def mm(a, b):
    return jnp.dot(a, b, preferred_element_type=F32)


def reorder(x, order):
    head, tail = (mm(piece, order).astype(BF16) for piece in split(x))
    return mm(order, head) + mm(order, tail)


def stack_rows(blocks):
    return jnp.concatenate(blocks, axis=0)


def stack_cols(blocks):
    return jnp.concatenate(blocks, axis=1)


def left_mul(x, table):
    half = x.shape[0]
    out = mm(table, stack_rows(split(x)))
    return out[:half] + out[half:]


def right_mul(x, table):
    half = x.shape[1]
    out = mm(stack_cols(split(x)), table)
    return out[:, :half] + out[:, half:]


def halves(x, axis):
    half = x.shape[axis] // 2
    return (x[:half], x[half:]) if axis == 0 else (x[:, :half], x[:, half:])


def one_side(waves, table, axis, sign):
    mul, stack = (left_mul, stack_rows) if axis == 0 else (right_mul, stack_cols)
    cos_table, sin_table = (table[2], table[3]) if axis == 0 else (table[0], table[1])
    parts = []
    for wave in waves:
        cos_part, sin_part = [], []
        for x in wave:
            a, b = halves(x, axis)
            cos_part.append(mul(a - b, cos_table))
            sin_part.append(mul(a + b, sin_table))
        parts.append((cos_part, sin_part))
    out = []
    for (cr, ci), (sr, si) in parts:
        if sign > 0:
            out.append((stack([si + cr, si - cr]), stack([ci - sr, -ci - sr])))
        else:
            out.append((stack([cr - si, -cr - si]), stack([sr + ci, sr - ci])))
    return out


def forward(waves, table):
    return one_side(one_side(waves, table, 0, 1), table, 1, 1)


def backward(waves, table):
    return one_side(one_side(waves, table, 0, -1), table, 1, -1)


class Window:
    def __init__(self, info, tile, slot, shape):
        slots = (info.shape[1] - 1) // 2
        rows = true_index(lax.broadcasted_iota(jnp.int32, shape, 0), shape[0])
        cols = true_index(lax.broadcasted_iota(jnp.int32, shape, 1), shape[1])
        is_live = slot < info[tile, 2 * slots]
        left = jnp.where(is_live, info[tile, 2 * slot + 1], 0 if tile else shape[1])
        self.low = rows < info[tile, 2 * slot]
        self.right = cols < left
        mine = self.right if tile else ~self.right
        self.keep_up = mine & ~self.low
        self.keep_low = mine & self.low

    def pick(self, quads, plane):
        own, east, south, corner = (q[plane, 0 : self.low.shape[0]] for q in quads)
        return jnp.where(self.low, jnp.where(self.right, corner, south), jnp.where(self.right, east, own))


def deposit(up, low, plane, windows, values):
    up[plane] += sum(jnp.where(w.keep_up, v, 0.0) for w, v in zip(windows, values))
    low[plane] += sum(jnp.where(w.keep_low, v, 0.0) for w, v in zip(windows, values))


def each_group(info, tile, body):
    slots = (info.shape[1] - 1) // 2
    group = 2 if slots % 2 == 0 else 1

    def step(g, carry):
        body([g * group + j for j in range(group)])
        return carry

    lax.fori_loop(0, (info[tile, 2 * slots] + group - 1) // group, step, 0)


def clear(*refs):
    for ref in refs:
        ref[...] = jnp.zeros_like(ref)


def shift_probe(info, tile, probe, ramp, shifted, up, low):
    shape = probe.shape[1:]
    rows = lax.broadcasted_iota(jnp.int32, shape, 0)
    cols = lax.broadcasted_iota(jnp.int32, shape, 1)

    def moved(position, source, offset):
        wanted = true_index(position, shape[0]) - offset
        wanted = jnp.where(wanted < 0, wanted + shape[0], wanted)
        return jnp.where(wanted == source, 1.0, 0.0).astype(BF16)

    def body(slots):
        windows, powers = [Window(info, tile, s, shape) for s in slots], []
        pieces = [split(probe[part]) for part in range(2)]
        for s in slots:
            to_cols = moved(cols, rows, info[tile, 2 * s + 1])
            to_rows = moved(rows, cols, info[tile, 2 * s])
            once = [[mm(piece, to_cols).astype(BF16) for piece in both] for both in pieces]
            pr, pi = (mm(to_rows, head) + mm(to_rows, tail) for head, tail in once)
            shifted[s, 0] = pr * ramp[0] - pi * ramp[1]
            shifted[s, 1] = pr * ramp[1] + pi * ramp[0]
            powers.append(pr * pr + pi * pi)
        deposit(up, low, 0, windows, powers)

    each_group(info, tile, body)


def cos_sin(angle):
    half = 0.5 * angle
    square = half * half

    def series(start):
        total, term = 0.0, []
        for k in range(7):
            term.append((-1.0) ** k / math.factorial(2 * k + start))
        for factor in reversed(term):
            total = factor + square * total
        return total

    sine, cosine = half * series(1), series(0)
    return 1.0 - 2.0 * sine * sine, 2.0 * sine * cosine


def own_prep_kernel(
    info, amp_in, probe_in, ramp_in, phase_in,
    shifted, amp, up, low, probe, ramp, phase, amp_sem, sem,
):
    amp_copies = [
        pltpu.make_async_copy(amp_in.at[s], amp.at[s], amp_sem.at[s]) for s in range(amp.shape[0])
    ]
    copies = [
        pltpu.make_async_copy(source, out, sem.at[k])
        for k, (source, out) in enumerate(((probe_in, probe), (ramp_in, ramp), (phase_in, phase)))
    ]
    for copy in amp_copies + copies:
        copy.start()
    clear(up, low)
    order = order_matrix(amp.shape[1])
    for copy in amp_copies:
        copy.wait()
    for s in range(amp.shape[0]):
        amp[s] = reorder(amp[s], order)
    for copy in copies:
        copy.wait()
    shift_probe(info, 0, probe, ramp, shifted, up, low)


def west_prep_kernel(
    own_info, probe, phase, ramp, west, up_in, low_in, up, low, shifted, phasor, info, note, sem
):
    copy = pltpu.make_async_copy(west.at[0, probe.shape[1] :, 0 : note.shape[1]], note, sem)
    copy.start()
    order = order_matrix(phase.shape[0])
    for part, value in enumerate(cos_sin(phase[...])):
        phasor[part] = reorder(value, order)
    copy.wait()
    for k in range(info.shape[1]):
        info[0, k] = own_info[0, k]
        info[1, k] = note[0, k].astype(jnp.int32)
    shift_probe(info, 1, probe, ramp, shifted, up, low)


def first_step(info, tile, slots, quads, shifted, phasor, table, wave, up, low):
    shape = up.shape[1:]
    windows = [Window(info, tile, s, shape) for s in slots]
    waves = []
    for s, w in zip(slots, windows):
        fr, fi = w.pick(quads, 0), w.pick(quads, 1)
        pr, pi = shifted[s, 0], shifted[s, 1]
        waves.append((pr * fr - pi * fi, pr * fi + pi * fr))
    waves = forward(waves, table)
    hr, hi = phasor[0], phasor[1]
    waves = backward([(ur * hr - ui * hi, ur * hi + ui * hr) for ur, ui in waves], table)
    for s, (wr, wi) in zip(slots, waves):
        wave[s, 0] = wr
        wave[s, 1] = wi
    deposit(up, low, 0, windows, [wr * wr + wi * wi for wr, wi in waves])


def first_kernel(
    info, own, east, south, corner, west, west_south, shifted, west_shifted, phasor, table,
    cover_up, cover_low, wave, west_wave, up, low,
):
    up[0] = jnp.zeros_like(up[0])
    low[0] = jnp.zeros_like(low[0])
    up[1] = cover_up[0]
    low[1] = cover_low[0]
    quads = (own, east, south.at[0:2], corner)
    each_group(
        info, 0, lambda s: first_step(info, 0, s, quads, shifted, phasor, table, wave, up, low)
    )
    west_quads = (west, own, west_south, south.at[0:2])
    each_group(
        info,
        1,
        lambda s: first_step(
            info, 1, s, west_quads, west_shifted, phasor, table, west_wave, up, low
        ),
    )


def second_step(info, tile, slots, quads, wave, amp, table, inner, up, low, picked):
    windows = [Window(info, tile, s, up.shape[1:]) for s in slots]
    waves = []
    for j, (s, w) in enumerate(zip(slots, windows)):
        sr, si = w.pick(quads, 0), w.pick(quads, 1)
        picked[j, 0] = sr
        picked[j, 1] = si
        wr, wi = wave[s, 0], wave[s, 1]
        waves.append((wr * sr - wi * si, wr * si + wi * sr))
    scaled = []
    for s, (fr, fi) in zip(slots, forward(waves, table)):
        ratio = amp[s] * lax.rsqrt(jnp.maximum(fr * fr + fi * fi, 0.25)) - 1.0
        scaled.append((fr * ratio, fi * ratio))
    real, imag = [], []
    for j, (s, (br, bi)) in enumerate(zip(slots, backward(scaled, table))):
        sr, si = picked[j, 0], picked[j, 1]
        inner[s, 0] = sr * br + si * bi
        inner[s, 1] = sr * bi - si * br
        wr, wi = wave[s, 0], wave[s, 1]
        real.append(wr * br + wi * bi)
        imag.append(wr * bi - wi * br)
    deposit(up, low, 0, windows, real)
    deposit(up, low, 1, windows, imag)


def third_step(info, tile, slots, inner, shifted, phasor, table, up, low):
    waves = forward([(inner[s, 0], inner[s, 1]) for s in slots], table)
    hr, hi = phasor[0], phasor[1]
    waves = backward([(tr * hr + ti * hi, ti * hr - tr * hi) for tr, ti in waves], table)
    windows = [Window(info, tile, s, up.shape[1:]) for s in slots]
    real, imag = [], []
    for s, (qr, qi) in zip(slots, waves):
        pr, pi = shifted[s, 0], shifted[s, 1]
        real.append(pr * qr + pi * qi)
        imag.append(pr * qi - pi * qr)
    deposit(up, low, 0, windows, real)
    deposit(up, low, 1, windows, imag)


def own_kernel(
    info, own, east, south, corner, wave, amp, shifted, phasor, table, up2, low2, up1, low1, inner, picked
):
    clear(up2, low2, up1, low1)
    quads = (own, east, south.at[2:4], corner)

    def body(slots):
        second_step(info, 0, slots, quads, wave, amp, table, inner, up2, low2, picked)
        third_step(info, 0, slots, inner, shifted, phasor, table, up1, low1)

    each_group(info, 0, body)


def west_second_kernel(
    info, own, south, west, west_south, wave, amp, table, up_in, low_in, up, low, inner, picked
):
    quads = (west, own, west_south, south.at[2:4])
    each_group(
        info,
        1,
        lambda slots: second_step(
            info, 1, slots, quads, wave, amp, table, inner, up, low, picked
        ),
    )


def west_third_kernel(info, inner, shifted, phasor, table, up_in, low_in, up, low):
    each_group(
        info, 1, lambda slots: third_step(info, 1, slots, inner, shifted, phasor, table, up, low)
    )


def load_kernel(coords_in, source, live, raw, first, second, whole, info, coords, coords_sem, sem):
    coords_copy = pltpu.make_async_copy(coords_in, coords, coords_sem)
    coords_copy.start()
    planes, rows, width = raw.shape
    copies = []
    for plane in range(planes):
        copies.append(pltpu.make_async_copy(source.at[plane], raw.at[plane], sem.at[plane]))
        copies[-1].start()
    order = order_matrix(width)
    coords_copy.wait()
    slots = coords.shape[-1]
    lane = lax.broadcasted_iota(jnp.int32, (NOTE_ROWS, width), 1)
    note = jnp.where(lane == 2 * slots, live[0, 0], 0)
    info[0, 2 * slots] = live[0, 0]
    for s in range(slots):
        for axis in range(2):
            info[0, 2 * s + axis] = coords[0, 0, axis, s]
            note = jnp.where(lane == 2 * s + axis, coords[0, 0, axis, s], note)
    for plane in range(first.shape[0]):
        first[plane, rows:] = note.astype(F32)
    for copy in copies:
        copy.wait()
    for plane in range(planes):
        ordered = reorder(raw[plane], order)
        whole[plane] = ordered
        if plane < 2:
            first[plane, 0:rows] = ordered
        else:
            second[plane - 2] = ordered


def load(coords, source, live):
    planes, rows, width = source.shape
    slots = coords.shape[-1]
    hbm = pl.BlockSpec(memory_space=pl.ANY)
    tile = (rows, width)
    return pl.pallas_call(
        load_kernel,
        out_shape=[
            pltpu.VMEM((planes,) + tile, F32),
            pltpu.VMEM((2, rows + NOTE_ROWS, width), F32),
            pltpu.VMEM((planes - 2,) + tile, F32),
            pltpu.VMEM((planes,) + tile, F32),
            jax.ShapeDtypeStruct((1, 2 * slots + 1), jnp.int32),
        ],
        in_specs=[hbm, hbm, SMEM],
        out_specs=[VMEM] * 4 + [SMEM],
        scratch_shapes=[
            pltpu.SMEM(coords.shape, jnp.int32),
            pltpu.SemaphoreType.DMA,
            pltpu.SemaphoreType.DMA((planes,)),
        ],
        compiler_params=pltpu.CompilerParams(vmem_limit_bytes=8 << 20),
        cost_estimate=pl.CostEstimate(flops=10**6, bytes_accessed=10**3, transcendentals=0),
    )(*(pltpu.with_memory_space_constraint(x, pltpu.HBM) for x in (coords, source)), live)


def update_kernel(planes, up, moved, power_up, power_moved, *refs, which, at):
    out, result, sem = refs[-3:]
    weight = 1.0 / (power_up[which] + power_moved[which] + 1.0)
    order = order_matrix(weight.shape[0])
    for part in range(up.shape[0]):
        result[part] = planes[at + part] + reorder((up[part] + moved[part]) * weight, order)
    copy = pltpu.make_async_copy(result, out.at[at : at + up.shape[0]], sem)
    copy.start()
    copy.wait()


def update(planes, up, moved, power_up, power_moved, which, at, before=None):
    shape = planes.shape
    operands = [planes, up, moved, power_up, power_moved]
    in_specs = [VMEM] * len(operands)
    aliases = {}
    if before is not None:
        aliases = {len(operands): 0}
        operands.append(before)
        in_specs.append(pl.BlockSpec(memory_space=pl.ANY))
    return pl.pallas_call(
        functools.partial(update_kernel, which=which, at=at),
        out_shape=pltpu.HBM(shape, F32),
        in_specs=in_specs,
        out_specs=pl.BlockSpec(memory_space=pl.ANY),
        input_output_aliases=aliases,
        scratch_shapes=[pltpu.VMEM(up.shape, F32), pltpu.SemaphoreType.DMA],
        compiler_params=pltpu.CompilerParams(vmem_limit_bytes=8 << 20),
        cost_estimate=pl.CostEstimate(flops=10**6, bytes_accessed=10**3, transcendentals=0),
    )(*operands)


def call(kernel, shapes, *operands, scratch=(), info_shape=None, add_to=0, in_hbm=0):
    operands = [
        pltpu.with_memory_space_constraint(x, pltpu.HBM) if 0 < k <= in_hbm else x
        for k, x in enumerate(operands)
    ]
    outs, out_specs = [pltpu.VMEM(s, F32) for s in shapes], [VMEM] * len(shapes)
    if info_shape is not None:
        outs.append(jax.ShapeDtypeStruct(info_shape, jnp.int32))
        out_specs.append(SMEM)
    return pl.pallas_call(
        kernel,
        out_shape=outs,
        in_specs=[SMEM]
        + [pl.BlockSpec(memory_space=pl.ANY)] * in_hbm
        + [VMEM] * (len(operands) - 1 - in_hbm),
        out_specs=out_specs,
        input_output_aliases={len(operands) - add_to + k: k for k in range(add_to)},
        scratch_shapes=scratch,
        compiler_params=pltpu.CompilerParams(vmem_limit_bytes=20 << 20),
        cost_estimate=pl.CostEstimate(flops=10**6, bytes_accessed=10**3, transcendentals=0),
    )(*operands)


def on_device(object_planes, probe, phase, coords, live, amplitude):
    width = probe.shape[-1]
    slots = coords.shape[2]
    tile = (width, width)
    pair = (2,) + tile
    one = (1,) + tile
    wave_shape = (slots,) + pair
    table = jnp.asarray(transform_tables(width))
    ramp = jnp.asarray(ramp_table(width))

    coords = jnp.swapaxes(coords, 2, 3)
    raw, first, second, whole, own_info = load(coords, object_planes, live)
    west1 = from_behind(first, "tx", 1)
    east1 = from_behind(first, "tx", -1)
    west2 = from_behind(second, "tx", 1)
    east2 = from_behind(second, "tx", -1)
    south = from_behind(whole, "ty", -1)

    shifted, amp, cover_up, cover_low, probe, ramp, phase = call(
        own_prep_kernel,
        [wave_shape, (slots,) + tile, one, one, pair, pair, tile],
        own_info, amplitude[0, 0], probe, ramp, phase,
        scratch=[pltpu.SemaphoreType.DMA((slots,)), pltpu.SemaphoreType.DMA((3,))],
        in_hbm=4,
    )
    east1, west1, table, shifted = lax.optimization_barrier((east1, west1, table, shifted))
    corner1 = from_behind(east1, "ty", -1)
    west_south1 = from_behind(west1, "ty", -1)
    cover_up, cover_low, west_shifted, phasor, info = call(
        west_prep_kernel,
        [one, one, wave_shape, pair],
        own_info, probe, phase, ramp, west1, cover_up, cover_low,
        add_to=2, info_shape=(2, 2 * slots + 1),
        scratch=[pltpu.SMEM((NOTE_ROWS, 128), F32), pltpu.SemaphoreType.DMA],
    )
    east2, west2, west_shifted = lax.optimization_barrier((east2, west2, west_shifted))
    corner2 = from_behind(east2, "ty", -1)
    moving, west2 = lax.optimization_barrier((amp, west2))
    amp_west = from_behind(moving, "tx", 1)
    west_south2 = from_behind(west2, "ty", -1)
    wave, west_wave, power_up, power_low = call(
        first_kernel,
        [wave_shape, wave_shape, pair, pair],
        info, first, east1, south, corner1, west1, west_south1,
        shifted, west_shifted, phasor, table, cover_up, cover_low,
    )
    power_moved = from_behind(power_low, "ty", 1)
    corner2, west_south2 = lax.optimization_barrier((corner2, west_south2))
    up2, low2, up1, low1 = call(
        own_kernel,
        [pair] * 4,
        info, second, east2, south, corner2, wave, amp, shifted, phasor, table,
        scratch=[pltpu.VMEM(wave_shape, F32), pltpu.VMEM((2,) + pair, F32)],
    )
    amp_west, power_moved = lax.optimization_barrier((amp_west, power_moved))
    up2, low2, inner = call(
        west_second_kernel,
        [pair, pair, wave_shape],
        info, second, south, west2, west_south2, west_wave, amp_west, table, up2, low2,
        scratch=[pltpu.VMEM((2,) + pair, F32)], add_to=2,
    )
    moved2 = from_behind(low2, "ty", 1)
    up1, low1 = call(
        west_third_kernel,
        [pair, pair],
        info, inner, west_shifted, phasor, table, up1, low1,
        add_to=2,
    )
    moved1 = from_behind(low1, "ty", 1)
    out = update(raw, up2, moved2, power_up, power_moved, 0, 2)
    return update(raw, up1, moved1, power_up, power_moved, 1, 0, out)


def solution(mesh):
    return jax.shard_map(
        on_device,
        mesh=mesh,
        in_specs=(
            P(None, ("groups", "ty"), "tx"),
            P(),
            P(),
            P(("groups", "ty"), "tx", None, None),
            P(("groups", "ty"), "tx"),
            P(("groups", "ty"), "tx", None, None, None),
        ),
        out_specs=P(None, ("groups", "ty"), "tx"),
        check_vma=False,
    )
```

```python
import functools
import math

import jax
import jax.numpy as jnp
import ml_dtypes
import numpy as np
from jax import lax
from jax.experimental import pallas as pl
from jax.experimental.pallas import tpu as pltpu
from jax.sharding import PartitionSpec as P

F32 = jnp.float32
BF16 = jnp.bfloat16
VMEM = pl.BlockSpec(memory_space=pltpu.VMEM)
NOTE_ROWS = 8
SMEM = pl.BlockSpec(memory_space=pltpu.SMEM)


def from_behind(block, axis, distance):
    devices = range(lax.axis_size(axis))
    route = [(i - distance, i) for i in devices if i - distance in devices]
    return lax.ppermute(block, axis, route)


def true_index(position, width):
    return jnp.where(position < width // 2, position, width + width // 2 - 1 - position)


def transform_tables(width):
    half = width // 2
    index = 2 * np.arange(half) + 1
    angle = 2.0 * math.pi * ((index[:, None] * index[None, :]) % (4 * width)) / (4 * width)
    out = []
    for real in (np.cos(angle), np.sin(angle)):
        real = real / math.sqrt(width)
        head = real.astype(ml_dtypes.bfloat16)
        tail = (real - head.astype(np.float64)).astype(ml_dtypes.bfloat16)
        out.append(np.block([[head, tail], [head, tail]]))
    out += [np.ascontiguousarray(m.T) for m in out]
    return np.stack(out)


def fold_index(width):
    return np.concatenate([np.arange(width // 2), np.arange(width // 2, width)[::-1]])


def order_matrix(width):
    rows = lax.broadcasted_iota(jnp.int32, (width, width), 0)
    cols = lax.broadcasted_iota(jnp.int32, (width, width), 1)
    return jnp.where(true_index(rows, width) == cols, 1.0, 0.0).astype(BF16)


def ramp_table(width):
    where = fold_index(width)
    angle = math.pi * (where[:, None] + where[None, :]) / width
    return np.stack([np.cos(angle), np.sin(angle)]).astype(np.float32)


def split(x):
    head = x.astype(BF16)
    return head, (x - head.astype(F32)).astype(BF16)


def mm(a, b):
    return jnp.dot(a, b, preferred_element_type=F32)


def reorder(x, order):
    head, tail = (mm(piece, order).astype(BF16) for piece in split(x))
    return mm(order, head) + mm(order, tail)


def stack_rows(blocks):
    return jnp.concatenate(blocks, axis=0)


def stack_cols(blocks):
    return jnp.concatenate(blocks, axis=1)


def left_mul(x, table):
    half = x.shape[0]
    out = mm(table, stack_rows(split(x)))
    return out[:half] + out[half:]


def right_mul(x, table):
    half = x.shape[1]
    out = mm(stack_cols(split(x)), table)
    return out[:, :half] + out[:, half:]


def halves(x, axis):
    half = x.shape[axis] // 2
    return (x[:half], x[half:]) if axis == 0 else (x[:, :half], x[:, half:])


def one_side(waves, table, axis, sign):
    mul, stack = (left_mul, stack_rows) if axis == 0 else (right_mul, stack_cols)
    cos_table, sin_table = (table[2], table[3]) if axis == 0 else (table[0], table[1])
    parts = []
    for wave in waves:
        cos_part, sin_part = [], []
        for x in wave:
            a, b = halves(x, axis)
            cos_part.append(mul(a - b, cos_table))
            sin_part.append(mul(a + b, sin_table))
        parts.append((cos_part, sin_part))
    out = []
    for (cr, ci), (sr, si) in parts:
        if sign > 0:
            out.append((stack([si + cr, si - cr]), stack([ci - sr, -ci - sr])))
        else:
            out.append((stack([cr - si, -cr - si]), stack([sr + ci, sr - ci])))
    return out


def forward(waves, table):
    return one_side(one_side(waves, table, 0, 1), table, 1, 1)


def backward(waves, table):
    return one_side(one_side(waves, table, 0, -1), table, 1, -1)


class Window:
    def __init__(self, info, tile, slot, shape):
        slots = (info.shape[1] - 1) // 2
        rows = true_index(lax.broadcasted_iota(jnp.int32, shape, 0), shape[0])
        cols = true_index(lax.broadcasted_iota(jnp.int32, shape, 1), shape[1])
        is_live = slot < info[tile, 2 * slots]
        left = jnp.where(is_live, info[tile, 2 * slot + 1], 0 if tile else shape[1])
        self.low = rows < info[tile, 2 * slot]
        self.right = cols < left
        mine = self.right if tile else ~self.right
        self.keep_up = mine & ~self.low
        self.keep_low = mine & self.low

    def pick(self, quads, plane):
        own, east, south, corner = (q[plane, 0 : self.low.shape[0]] for q in quads)
        return jnp.where(self.low, jnp.where(self.right, corner, south), jnp.where(self.right, east, own))


def deposit(up, low, plane, windows, values):
    up[plane] += sum(jnp.where(w.keep_up, v, 0.0) for w, v in zip(windows, values))
    low[plane] += sum(jnp.where(w.keep_low, v, 0.0) for w, v in zip(windows, values))


def each_group(info, tile, body):
    slots = (info.shape[1] - 1) // 2
    group = 2 if slots % 2 == 0 else 1

    def step(g, carry):
        body([g * group + j for j in range(group)])
        return carry

    lax.fori_loop(0, (info[tile, 2 * slots] + group - 1) // group, step, 0)


def clear(*refs):
    for ref in refs:
        ref[...] = jnp.zeros_like(ref)


def shift_probe(info, tile, probe, ramp, shifted, up, low):
    shape = probe.shape[1:]
    rows = lax.broadcasted_iota(jnp.int32, shape, 0)
    cols = lax.broadcasted_iota(jnp.int32, shape, 1)

    def moved(position, source, offset):
        wanted = true_index(position, shape[0]) - offset
        wanted = jnp.where(wanted < 0, wanted + shape[0], wanted)
        return jnp.where(wanted == source, 1.0, 0.0).astype(BF16)

    def body(slots):
        windows, powers = [Window(info, tile, s, shape) for s in slots], []
        pieces = [split(probe[part]) for part in range(2)]
        for s in slots:
            to_cols = moved(cols, rows, info[tile, 2 * s + 1])
            to_rows = moved(rows, cols, info[tile, 2 * s])
            once = [[mm(piece, to_cols).astype(BF16) for piece in both] for both in pieces]
            pr, pi = (mm(to_rows, head) + mm(to_rows, tail) for head, tail in once)
            shifted[s, 0] = pr * ramp[0] - pi * ramp[1]
            shifted[s, 1] = pr * ramp[1] + pi * ramp[0]
            powers.append(pr * pr + pi * pi)
        deposit(up, low, 0, windows, powers)

    each_group(info, tile, body)


def cos_sin(angle):
    half = 0.5 * angle
    square = half * half

    def series(start):
        total, term = 0.0, []
        for k in range(7):
            term.append((-1.0) ** k / math.factorial(2 * k + start))
        for factor in reversed(term):
            total = factor + square * total
        return total

    sine, cosine = half * series(1), series(0)
    return 1.0 - 2.0 * sine * sine, 2.0 * sine * cosine


def own_prep_kernel(
    info, amp_in, probe_in, ramp_in, phase_in,
    shifted, amp, up, low, probe, ramp, phase, amp_sem, sem,
):
    amp_copies = [
        pltpu.make_async_copy(amp_in.at[s], amp.at[s], amp_sem.at[s]) for s in range(amp.shape[0])
    ]
    copies = [
        pltpu.make_async_copy(source, out, sem.at[k])
        for k, (source, out) in enumerate(((probe_in, probe), (ramp_in, ramp), (phase_in, phase)))
    ]
    for copy in copies + amp_copies:
        copy.start()
    clear(up, low)
    order = order_matrix(amp.shape[1])
    for copy in copies:
        copy.wait()
    shift_probe(info, 0, probe, ramp, shifted, up, low)
    for copy in amp_copies:
        copy.wait()
    for s in range(amp.shape[0]):
        amp[s] = reorder(amp[s], order)


def west_prep_kernel(
    own_info, probe, phase, ramp, west, up_in, low_in, up, low, shifted, phasor, info, note, sem
):
    copy = pltpu.make_async_copy(west.at[0, probe.shape[1] :, 0 : note.shape[1]], note, sem)
    copy.start()
    order = order_matrix(phase.shape[0])
    for part, value in enumerate(cos_sin(phase[...])):
        phasor[part] = reorder(value, order)
    copy.wait()
    for k in range(info.shape[1]):
        info[0, k] = own_info[0, k]
        info[1, k] = note[0, k].astype(jnp.int32)
    shift_probe(info, 1, probe, ramp, shifted, up, low)


def first_step(info, tile, slots, quads, shifted, phasor, table, wave, up, low):
    shape = up.shape[1:]
    windows = [Window(info, tile, s, shape) for s in slots]
    waves = []
    for s, w in zip(slots, windows):
        fr, fi = w.pick(quads, 0), w.pick(quads, 1)
        pr, pi = shifted[s, 0], shifted[s, 1]
        waves.append((pr * fr - pi * fi, pr * fi + pi * fr))
    waves = forward(waves, table)
    hr, hi = phasor[0], phasor[1]
    waves = backward([(ur * hr - ui * hi, ur * hi + ui * hr) for ur, ui in waves], table)
    for s, (wr, wi) in zip(slots, waves):
        wave[s, 0] = wr
        wave[s, 1] = wi
    deposit(up, low, 0, windows, [wr * wr + wi * wi for wr, wi in waves])


def first_kernel(
    info, own, east, south, corner, west, west_south, shifted, west_shifted, phasor, table,
    cover_up, cover_low, wave, west_wave, up, low,
):
    up[0] = jnp.zeros_like(up[0])
    low[0] = jnp.zeros_like(low[0])
    up[1] = cover_up[0]
    low[1] = cover_low[0]
    quads = (own, east, south.at[0:2], corner)
    each_group(
        info, 0, lambda s: first_step(info, 0, s, quads, shifted, phasor, table, wave, up, low)
    )
    west_quads = (west, own, west_south, south.at[0:2])
    each_group(
        info,
        1,
        lambda s: first_step(
            info, 1, s, west_quads, west_shifted, phasor, table, west_wave, up, low
        ),
    )


def second_step(info, tile, slots, quads, wave, amp, table, inner, up, low, picked):
    windows = [Window(info, tile, s, up.shape[1:]) for s in slots]
    waves = []
    for j, (s, w) in enumerate(zip(slots, windows)):
        sr, si = w.pick(quads, 0), w.pick(quads, 1)
        picked[j, 0] = sr
        picked[j, 1] = si
        wr, wi = wave[s, 0], wave[s, 1]
        waves.append((wr * sr - wi * si, wr * si + wi * sr))
    scaled = []
    for s, (fr, fi) in zip(slots, forward(waves, table)):
        ratio = amp[s] * lax.rsqrt(jnp.maximum(fr * fr + fi * fi, 0.25)) - 1.0
        scaled.append((fr * ratio, fi * ratio))
    real, imag = [], []
    for j, (s, (br, bi)) in enumerate(zip(slots, backward(scaled, table))):
        sr, si = picked[j, 0], picked[j, 1]
        inner[s, 0] = sr * br + si * bi
        inner[s, 1] = sr * bi - si * br
        wr, wi = wave[s, 0], wave[s, 1]
        real.append(wr * br + wi * bi)
        imag.append(wr * bi - wi * br)
    deposit(up, low, 0, windows, real)
    deposit(up, low, 1, windows, imag)


def third_step(info, tile, slots, inner, shifted, phasor, table, up, low):
    waves = forward([(inner[s, 0], inner[s, 1]) for s in slots], table)
    hr, hi = phasor[0], phasor[1]
    waves = backward([(tr * hr + ti * hi, ti * hr - tr * hi) for tr, ti in waves], table)
    windows = [Window(info, tile, s, up.shape[1:]) for s in slots]
    real, imag = [], []
    for s, (qr, qi) in zip(slots, waves):
        pr, pi = shifted[s, 0], shifted[s, 1]
        real.append(pr * qr + pi * qi)
        imag.append(pr * qi - pi * qr)
    deposit(up, low, 0, windows, real)
    deposit(up, low, 1, windows, imag)


def own_kernel(
    info, own, east, south, corner, wave, amp, shifted, phasor, table, up2, low2, up1, low1, inner, picked
):
    clear(up2, low2, up1, low1)
    quads = (own, east, south.at[2:4], corner)

    def body(slots):
        second_step(info, 0, slots, quads, wave, amp, table, inner, up2, low2, picked)
        third_step(info, 0, slots, inner, shifted, phasor, table, up1, low1)

    each_group(info, 0, body)


def west_second_kernel(
    info, own, south, west, west_south, wave, amp, table, up_in, low_in, up, low, inner, picked
):
    quads = (west, own, west_south, south.at[2:4])
    each_group(
        info,
        1,
        lambda slots: second_step(
            info, 1, slots, quads, wave, amp, table, inner, up, low, picked
        ),
    )


def west_third_kernel(info, inner, shifted, phasor, table, up_in, low_in, up, low):
    each_group(
        info, 1, lambda slots: third_step(info, 1, slots, inner, shifted, phasor, table, up, low)
    )


def load_kernel(coords_in, source, live, raw, first, second, whole, info, coords, coords_sem, sem):
    coords_copy = pltpu.make_async_copy(coords_in, coords, coords_sem)
    coords_copy.start()
    planes, rows, width = raw.shape
    copies = []
    for plane in range(planes):
        copies.append(pltpu.make_async_copy(source.at[plane], raw.at[plane], sem.at[plane]))
        copies[-1].start()
    order = order_matrix(width)
    coords_copy.wait()
    slots = coords.shape[-1]
    lane = lax.broadcasted_iota(jnp.int32, (NOTE_ROWS, width), 1)
    note = jnp.where(lane == 2 * slots, live[0, 0], 0)
    info[0, 2 * slots] = live[0, 0]
    for s in range(slots):
        for axis in range(2):
            info[0, 2 * s + axis] = coords[0, 0, axis, s]
            note = jnp.where(lane == 2 * s + axis, coords[0, 0, axis, s], note)
    for plane in range(first.shape[0]):
        first[plane, rows:] = note.astype(F32)
    for copy in copies:
        copy.wait()
    for plane in range(planes):
        ordered = reorder(raw[plane], order)
        whole[plane] = ordered
        if plane < 2:
            first[plane, 0:rows] = ordered
        else:
            second[plane - 2] = ordered


def load(coords, source, live):
    planes, rows, width = source.shape
    slots = coords.shape[-1]
    hbm = pl.BlockSpec(memory_space=pl.ANY)
    tile = (rows, width)
    return pl.pallas_call(
        load_kernel,
        out_shape=[
            pltpu.VMEM((planes,) + tile, F32),
            pltpu.VMEM((2, rows + NOTE_ROWS, width), F32),
            pltpu.VMEM((planes - 2,) + tile, F32),
            pltpu.VMEM((planes,) + tile, F32),
            jax.ShapeDtypeStruct((1, 2 * slots + 1), jnp.int32),
        ],
        in_specs=[hbm, hbm, SMEM],
        out_specs=[VMEM] * 4 + [SMEM],
        scratch_shapes=[
            pltpu.SMEM(coords.shape, jnp.int32),
            pltpu.SemaphoreType.DMA,
            pltpu.SemaphoreType.DMA((planes,)),
        ],
        compiler_params=pltpu.CompilerParams(vmem_limit_bytes=8 << 20),
        cost_estimate=pl.CostEstimate(flops=10**6, bytes_accessed=10**3, transcendentals=0),
    )(*(pltpu.with_memory_space_constraint(x, pltpu.HBM) for x in (coords, source)), live)


def update_kernel(planes, up, moved, power_up, power_moved, *refs, which, at):
    out, result, sem = refs[-3:]
    weight = 1.0 / (power_up[which] + power_moved[which] + 1.0)
    order = order_matrix(weight.shape[0])
    copies = []
    for part in range(up.shape[0]):
        result[part] = planes[at + part] + reorder((up[part] + moved[part]) * weight, order)
        copies.append(pltpu.make_async_copy(result.at[part], out.at[at + part], sem.at[part]))
        copies[-1].start()
    for copy in copies:
        copy.wait()


def update(planes, up, moved, power_up, power_moved, which, at, before=None):
    shape = planes.shape
    operands = [planes, up, moved, power_up, power_moved]
    in_specs = [VMEM] * len(operands)
    aliases = {}
    if before is not None:
        aliases = {len(operands): 0}
        operands.append(before)
        in_specs.append(pl.BlockSpec(memory_space=pl.ANY))
    return pl.pallas_call(
        functools.partial(update_kernel, which=which, at=at),
        out_shape=pltpu.HBM(shape, F32),
        in_specs=in_specs,
        out_specs=pl.BlockSpec(memory_space=pl.ANY),
        input_output_aliases=aliases,
        scratch_shapes=[pltpu.VMEM(up.shape, F32), pltpu.SemaphoreType.DMA((up.shape[0],))],
        compiler_params=pltpu.CompilerParams(vmem_limit_bytes=8 << 20),
        cost_estimate=pl.CostEstimate(flops=10**6, bytes_accessed=10**3, transcendentals=0),
    )(*operands)


def call(kernel, shapes, *operands, scratch=(), info_shape=None, add_to=0, in_hbm=0):
    operands = [
        pltpu.with_memory_space_constraint(x, pltpu.HBM) if 0 < k <= in_hbm else x
        for k, x in enumerate(operands)
    ]
    outs, out_specs = [pltpu.VMEM(s, F32) for s in shapes], [VMEM] * len(shapes)
    if info_shape is not None:
        outs.append(jax.ShapeDtypeStruct(info_shape, jnp.int32))
        out_specs.append(SMEM)
    return pl.pallas_call(
        kernel,
        out_shape=outs,
        in_specs=[SMEM]
        + [pl.BlockSpec(memory_space=pl.ANY)] * in_hbm
        + [VMEM] * (len(operands) - 1 - in_hbm),
        out_specs=out_specs,
        input_output_aliases={len(operands) - add_to + k: k for k in range(add_to)},
        scratch_shapes=scratch,
        compiler_params=pltpu.CompilerParams(vmem_limit_bytes=20 << 20),
        cost_estimate=pl.CostEstimate(flops=10**6, bytes_accessed=10**3, transcendentals=0),
    )(*operands)


def on_device(object_planes, probe, phase, coords, live, amplitude):
    width = probe.shape[-1]
    slots = coords.shape[2]
    tile = (width, width)
    pair = (2,) + tile
    one = (1,) + tile
    wave_shape = (slots,) + pair
    table = jnp.asarray(transform_tables(width))
    ramp = jnp.asarray(ramp_table(width))

    coords = jnp.swapaxes(coords, 2, 3)
    raw, first, second, whole, own_info = load(coords, object_planes, live)
    west1 = from_behind(first, "tx", 1)
    east1 = from_behind(first, "tx", -1)
    west2 = from_behind(second, "tx", 1)
    east2 = from_behind(second, "tx", -1)
    south = from_behind(whole, "ty", -1)

    shifted, amp, cover_up, cover_low, probe, ramp, phase = call(
        own_prep_kernel,
        [wave_shape, (slots,) + tile, one, one, pair, pair, tile],
        own_info, amplitude[0, 0], probe, ramp, phase,
        scratch=[pltpu.SemaphoreType.DMA((slots,)), pltpu.SemaphoreType.DMA((3,))],
        in_hbm=4,
    )
    east1, west1, table, shifted = lax.optimization_barrier((east1, west1, table, shifted))
    corner1 = from_behind(east1, "ty", -1)
    west_south1 = from_behind(west1, "ty", -1)
    cover_up, cover_low, west_shifted, phasor, info = call(
        west_prep_kernel,
        [one, one, wave_shape, pair],
        own_info, probe, phase, ramp, west1, cover_up, cover_low,
        add_to=2, info_shape=(2, 2 * slots + 1),
        scratch=[pltpu.SMEM((NOTE_ROWS, 128), F32), pltpu.SemaphoreType.DMA],
    )
    east2, west2, west_shifted = lax.optimization_barrier((east2, west2, west_shifted))
    corner2 = from_behind(east2, "ty", -1)
    moving, west2 = lax.optimization_barrier((amp, west2))
    amp_west = from_behind(moving, "tx", 1)
    west_south2 = from_behind(west2, "ty", -1)
    wave, west_wave, power_up, power_low = call(
        first_kernel,
        [wave_shape, wave_shape, pair, pair],
        info, first, east1, south, corner1, west1, west_south1,
        shifted, west_shifted, phasor, table, cover_up, cover_low,
    )
    power_moved = from_behind(power_low, "ty", 1)
    corner2, west_south2 = lax.optimization_barrier((corner2, west_south2))
    up2, low2, up1, low1 = call(
        own_kernel,
        [pair] * 4,
        info, second, east2, south, corner2, wave, amp, shifted, phasor, table,
        scratch=[pltpu.VMEM(wave_shape, F32), pltpu.VMEM((2,) + pair, F32)],
    )
    amp_west, power_moved = lax.optimization_barrier((amp_west, power_moved))
    up2, low2, inner = call(
        west_second_kernel,
        [pair, pair, wave_shape],
        info, second, south, west2, west_south2, west_wave, amp_west, table, up2, low2,
        scratch=[pltpu.VMEM((2,) + pair, F32)], add_to=2,
    )
    moved2 = from_behind(low2, "ty", 1)
    up1, low1 = call(
        west_third_kernel,
        [pair, pair],
        info, inner, west_shifted, phasor, table, up1, low1,
        add_to=2,
    )
    moved1 = from_behind(low1, "ty", 1)
    out = update(raw, up2, moved2, power_up, power_moved, 0, 2)
    return update(raw, up1, moved1, power_up, power_moved, 1, 0, out)


def solution(mesh):
    return jax.shard_map(
        on_device,
        mesh=mesh,
        in_specs=(
            P(None, ("groups", "ty"), "tx"),
            P(),
            P(),
            P(("groups", "ty"), "tx", None, None),
            P(("groups", "ty"), "tx"),
            P(("groups", "ty"), "tx", None, None, None),
        ),
        out_specs=P(None, ("groups", "ty"), "tx"),
        check_vma=False,
    )
```
